128 devices in a mesh: seq: 8 (over y_hi, z), res: 16 (over y_lo, x, core).
Axes of the slice: x: 4, y: 4 (y_hi: 2, y_lo: 2; y = y_hi * 2 + y_lo), z: 4, core: 2. Of those that a mesh axis runs over, the one named last changes fastest.
Arguments:
- homology_table: bfloat16 [64, 2560, 256], P('seq', 'res'), may hold values from -6 to 6
- coupled_state: bfloat16 [2560, 2560, 128], P('seq', 'res'), may hold values from -6 to 6
- aligned_indicator: int32 [64, 2560], P('seq', 'res'), may hold values 0 or 1
- amino_indicator: int32 [2560], P('res'), may hold values 0 or 1
- horizontal_scaling_factor: float32 [256], replicated, may hold values from 0.25 to 1.75
- horizontal_projection_matrix: bfloat16 [256, 1024], replicated, may hold values from -6 to 6
- horizontal_sigmoid_shift: float32 [256], replicated, may hold values from -6 to 6
- horizontal_result_matrix: bfloat16 [256, 256], replicated, may hold values from -0.375 to 0.375
- horizontal_result_shift: float32 [256], replicated, may hold values from -3 to 3
- coupling_scaling_factor: float32 [128], replicated, may hold values from 0.25 to 1.75
- coupling_head_matrix: bfloat16 [128, 8], replicated, may hold values from -2 to 2
- downward_stretch_vector: float32 [256], replicated, may hold values from 0.25 to 1.75
- vertical_projection_matrix: bfloat16 [256, 1024], replicated, may hold values from -6 to 6
- vertical_sigmoid_shift: float32 [256], replicated, may hold values from -6 to 6
- vertical_result_matrix: bfloat16 [256, 256], replicated, may hold values from -0.375 to 0.375
- vertical_result_shift: float32 [256], replicated, may hold values from -3 to 3
- feedforward_scaling_factor: float32 [256], replicated, may hold values from 0.25 to 1.75
- feedforward_expand_matrix: bfloat16 [256, 1024], replicated, may hold values from -0.375 to 0.375
- feedforward_shrink_matrix: bfloat16 [1024, 256], replicated, may hold values from -0.1875 to 0.1875
Outputs:
- updated: bfloat16 [64, 2560, 256], P('seq', 'res')
The draws below stay inside these ranges and needn't reach their ends.
All inputs are finite; a program needn't handle non-finite values. No bound on the sum of `aligned_indicator` or of `amino_indicator` on one device may be relied on, other than what follows from the above.
Results may differ from the reference program's by a relative error of at most 0.025.
Values may be sent and summed in bfloat16 or wider, within the bound.
No kernel may reach another device: no remote copies, remote signals or barrier semaphores. Data moves between devices by JAX's collectives and lax.ppermute only.
A program may use at most 256 MiB of HBM per device.

```python
import math
import jax
import jax.numpy as jnp
from jax import lax

CM = 256
CZ = 128
H = 8
DH = 32
TRANS = 1024
SEQUENCE_COUNT = 64
RESIDUE_COUNT = 2560
N_SEQ = 8


def repeated_entries(key, baseline, jitter_scale):
    subkeys = jax.random.split(key, 8)
    row_source = jax.random.randint(subkeys[0], (SEQUENCE_COUNT,), 0, SEQUENCE_COUNT)
    row_copied = (jax.random.randint(subkeys[1], (SEQUENCE_COUNT,), 0, 8) == 0) | (jnp.arange(SEQUENCE_COUNT) == jax.random.randint(subkeys[2], (), 0, SEQUENCE_COUNT))
    row_jitter = jitter_scale * jax.random.uniform(subkeys[3], (SEQUENCE_COUNT, RESIDUE_COUNT, CM), jnp.float32, -1.0, 1.0)
    blended = jnp.where(row_copied[:, None, None], baseline[row_source] + row_jitter, baseline)
    res_source = jax.random.randint(subkeys[4], (RESIDUE_COUNT,), 0, RESIDUE_COUNT)
    res_copied = (jax.random.randint(subkeys[5], (RESIDUE_COUNT,), 0, 16) == 0) | (jnp.arange(RESIDUE_COUNT) == jax.random.randint(subkeys[6], (), 0, RESIDUE_COUNT))
    res_jitter = jitter_scale * jax.random.uniform(subkeys[7], (SEQUENCE_COUNT, RESIDUE_COUNT, CM), jnp.float32, -1.0, 1.0)
    blended = jnp.where(res_copied[None, :, None], blended[:, res_source] + res_jitter, blended)
    return jnp.clip(blended, -6.0, 6.0)


def draw_homology_table(key, part):
    key = jax.random.fold_in(key, 7)
    subkeys = jax.random.split(key, 3)
    baseline = jnp.clip(jax.random.normal(subkeys[0], (SEQUENCE_COUNT, RESIDUE_COUNT, CM), jnp.float32), -6.0, 6.0)
    return repeated_entries(subkeys[2], baseline, 0.03).astype(jnp.bfloat16)


def projection(key, query_std, key_std, other_std):
    subkeys = jax.random.split(key, 4)
    queries = jnp.clip(jax.random.normal(subkeys[0], (CM, CM), jnp.float32), -6.0, 6.0) * query_std
    jitter = jnp.clip(jax.random.normal(subkeys[2], (CM, CM), jnp.float32), -6.0, 6.0) * key_std
    keys_block = jitter
    remaining = jnp.clip(jax.random.normal(subkeys[3], (CM, 2 * CM), jnp.float32), -6.0, 6.0) * other_std
    return jnp.clip(jnp.concatenate([queries, keys_block, remaining], axis=1), -6.0, 6.0)


def draw_horizontal_projection_matrix(key, part):
    key = jax.random.fold_in(key, 21)
    drawn_std = (CM // 2) ** (-0.5)
    return projection(key, drawn_std, drawn_std, drawn_std).astype(jnp.bfloat16)


def draw_vertical_projection_matrix(key, part):
    key = jax.random.fold_in(key, 33)
    drawn_std = (CM // 4) ** (-0.5)
    return projection(key, drawn_std, drawn_std, drawn_std).astype(jnp.bfloat16)


def place_ends(array, key, low, high):
    longest = array.shape.index(max(array.shape))
    spots = []
    for shift in (0, 1):
        where = [jax.random.randint(jax.random.fold_in(key, axis), (), 0, length) for axis, length in enumerate(array.shape)]
        where[longest] = (where[longest] + shift) % array.shape[longest]
        spots.append(tuple(where))
    return array.at[spots[0]].set(low).at[spots[1]].set(high)


def steps_of(key, dims, shards, smallest, largest):
    level = 1.0
    for dim, parts in shards:
        steps = jax.random.uniform(jax.random.fold_in(jax.random.fold_in(key, 6), dim), (parts,), jnp.float32, smallest / len(shards), largest / len(shards))
        level = level * jnp.repeat(jnp.exp(steps), dims[dim] // parts).reshape((-1,) + (1,) * (len(dims) - 1 - dim))
    return level


def scatter_about(own_key, extent, deviation, reach, cuts=(), kind=jnp.bfloat16):
    level = steps_of(own_key, extent, cuts, -0.22, 0.18) if cuts else 1.0
    array = jax.random.normal(own_key, extent, jnp.float32) * deviation * level
    return jnp.minimum(jnp.maximum(array, -reach), reach).astype(kind)


def setup_inputs(seed: int = 0) -> dict:
    splits = jax.random.split(jax.random.key(seed), 20)
    homology_table = draw_homology_table(jax.random.fold_in(splits[19], 71), 0)
    coupled_state = scatter_about(splits[1], (RESIDUE_COUNT, RESIDUE_COUNT, CZ), 1.0, 6.0, ((0, 8), (1, 16)))
    aligned_indicator = place_ends((jax.random.randint(splits[2], (SEQUENCE_COUNT, RESIDUE_COUNT), 0, 8) < 7).astype(jnp.int32), jax.random.fold_in(splits[2], 1), 0, 1)
    amino_indicator = place_ends((jax.random.randint(splits[3], (RESIDUE_COUNT,), 0, 16) < 15).astype(jnp.int32), jax.random.fold_in(splits[3], 1), 0, 1)
    horizontal_scaling_factor = jnp.clip(1.0 + 0.15 * jax.random.normal(splits[4], (CM,), jnp.float32), 0.25, 1.75)
    horizontal_projection_matrix = draw_horizontal_projection_matrix(jax.random.fold_in(splits[19], 71), 0)
    horizontal_sigmoid_shift = scatter_about(splits[6], (CM,), 1.0, 6.0, (), jnp.float32)
    horizontal_result_matrix = scatter_about(splits[7], (CM, CM), CM ** -0.5, 0.375)
    horizontal_result_shift = scatter_about(splits[8], (CM,), 0.5, 3.0, (), jnp.float32)
    coupling_scaling_factor = jnp.clip(1.0 + 0.15 * jax.random.normal(splits[9], (CZ,), jnp.float32), 0.25, 1.75)
    coupling_head_matrix = scatter_about(splits[10], (CZ, H), (CZ // 16) ** -0.5, 2.0)
    downward_stretch_vector = jnp.clip(1.0 + 0.15 * jax.random.normal(splits[11], (CM,), jnp.float32), 0.25, 1.75)
    vertical_projection_matrix = draw_vertical_projection_matrix(jax.random.fold_in(splits[19], 71), 0)
    vertical_sigmoid_shift = scatter_about(splits[13], (CM,), 1.0, 6.0, (), jnp.float32)
    vertical_result_matrix = scatter_about(splits[14], (CM, CM), CM ** -0.5, 0.375)
    vertical_result_shift = scatter_about(splits[15], (CM,), 0.5, 3.0, (), jnp.float32)
    feedforward_scaling_factor = jnp.clip(1.0 + 0.15 * jax.random.normal(splits[16], (CM,), jnp.float32), 0.25, 1.75)
    feedforward_expand_matrix = scatter_about(splits[17], (CM, TRANS), CM ** -0.5, 0.375)
    feedforward_shrink_matrix = scatter_about(splits[18], (TRANS, CM), TRANS ** -0.5, 0.1875)
    return {"homology_table": homology_table, "coupled_state": coupled_state, "aligned_indicator": aligned_indicator, "amino_indicator": amino_indicator, "horizontal_scaling_factor": horizontal_scaling_factor, "horizontal_projection_matrix": horizontal_projection_matrix, "horizontal_sigmoid_shift": horizontal_sigmoid_shift, "horizontal_result_matrix": horizontal_result_matrix, "horizontal_result_shift": horizontal_result_shift, "coupling_scaling_factor": coupling_scaling_factor, "coupling_head_matrix": coupling_head_matrix, "downward_stretch_vector": downward_stretch_vector, "vertical_projection_matrix": vertical_projection_matrix, "vertical_sigmoid_shift": vertical_sigmoid_shift, "vertical_result_matrix": vertical_result_matrix, "vertical_result_shift": vertical_result_shift, "feedforward_scaling_factor": feedforward_scaling_factor, "feedforward_expand_matrix": feedforward_expand_matrix, "feedforward_shrink_matrix": feedforward_shrink_matrix}


def normalize_lanes(values, gain):
    values = values.astype(jnp.float32)
    center = values - lax.optimization_barrier(jnp.mean(values, axis=-1, keepdims=True))
    spread = lax.optimization_barrier(jnp.mean(center * center, axis=-1, keepdims=True))
    return center * lax.rsqrt(spread + 1e-05) * gain

def reference(homology_table, coupled_state, aligned_indicator, amino_indicator, horizontal_scaling_factor, horizontal_projection_matrix, horizontal_sigmoid_shift, horizontal_result_matrix, horizontal_result_shift, coupling_scaling_factor, coupling_head_matrix, downward_stretch_vector, vertical_projection_matrix, vertical_sigmoid_shift, vertical_result_matrix, vertical_result_shift, feedforward_scaling_factor, feedforward_expand_matrix, feedforward_shrink_matrix):
    scale = 1.0 / math.sqrt(DH)
    blocks = coupled_state.reshape(N_SEQ, RESIDUE_COUNT // N_SEQ, RESIDUE_COUNT, CZ)

    def bias_block(rows):
        normed = normalize_lanes(rows, coupling_scaling_factor).astype(jnp.bfloat16)
        return jnp.einsum('ijc,ch->hij', normed.astype(jnp.float32), coupling_head_matrix.astype(jnp.float32)).astype(jnp.bfloat16)
    bias = lax.map(bias_block, blocks)
    bias = jnp.transpose(bias, (1, 0, 2, 3)).reshape(H, RESIDUE_COUNT, RESIDUE_COUNT)
    horizontal_standardized_state = normalize_lanes(homology_table, horizontal_scaling_factor).astype(jnp.bfloat16)
    proj = jnp.dot(horizontal_standardized_state.reshape(SEQUENCE_COUNT * RESIDUE_COUNT, CM), horizontal_projection_matrix, preferred_element_type=jnp.float32).reshape(SEQUENCE_COUNT, RESIDUE_COUNT, 4 * CM)
    row_q = proj[..., :CM].astype(jnp.bfloat16)
    row_k = proj[..., CM:2 * CM].astype(jnp.bfloat16)
    row_v = proj[..., 2 * CM:3 * CM].astype(jnp.bfloat16)
    row_gate = jax.nn.sigmoid(proj[..., 3 * CM:] + horizontal_sigmoid_shift)
    key_present_mask = aligned_indicator * amino_indicator[None, :]

    def one_row(items):
        query, keys, vals, mask_row = items
        attention_logits = jnp.einsum('qhd,khd->hqk', query.reshape(RESIDUE_COUNT, H, DH).astype(jnp.float32), keys.reshape(RESIDUE_COUNT, H, DH).astype(jnp.float32)) * scale + bias.astype(jnp.float32)
        attention_logits = jnp.where(mask_row[None, None, :] > 0, attention_logits, -1000000000.0)
        weights = jax.nn.softmax(attention_logits, axis=-1).astype(jnp.bfloat16)
        return jnp.einsum('hqk,khd->qhd', weights.astype(jnp.float32), vals.reshape(RESIDUE_COUNT, H, DH).astype(jnp.float32)).reshape(RESIDUE_COUNT, CM)
    row_o = lax.map(one_row, (row_q, row_k, row_v, key_present_mask))
    row_gated = (row_o * row_gate).astype(jnp.bfloat16)
    lateral_addend = jnp.dot(row_gated.reshape(SEQUENCE_COUNT * RESIDUE_COUNT, CM), horizontal_result_matrix, preferred_element_type=jnp.float32).reshape(SEQUENCE_COUNT, RESIDUE_COUNT, CM) + horizontal_result_shift
    homology_table_refreshed = (homology_table.astype(jnp.float32) + lateral_addend).astype(jnp.bfloat16)
    downward_source = normalize_lanes(homology_table_refreshed, downward_stretch_vector).astype(jnp.bfloat16)
    proj2 = jnp.dot(downward_source.reshape(SEQUENCE_COUNT * RESIDUE_COUNT, CM), vertical_projection_matrix, preferred_element_type=jnp.float32).reshape(SEQUENCE_COUNT, RESIDUE_COUNT, 4 * CM)
    col_q = proj2[..., :CM].astype(jnp.bfloat16).reshape(SEQUENCE_COUNT, RESIDUE_COUNT, H, DH)
    col_k = proj2[..., CM:2 * CM].astype(jnp.bfloat16).reshape(SEQUENCE_COUNT, RESIDUE_COUNT, H, DH)
    col_v = proj2[..., 2 * CM:3 * CM].astype(jnp.bfloat16).reshape(SEQUENCE_COUNT, RESIDUE_COUNT, H, DH)
    col_gate = jax.nn.sigmoid(proj2[..., 3 * CM:] + vertical_sigmoid_shift)
    attention_logits = jnp.einsum('sihd,tihd->ihst', col_q.astype(jnp.float32), col_k.astype(jnp.float32)) * scale
    attention_logits = jnp.where(jnp.transpose(aligned_indicator)[:, None, None, :] > 0, attention_logits, -1000000000.0)
    weights = jax.nn.softmax(attention_logits, axis=-1).astype(jnp.bfloat16)
    col_o = jnp.einsum('ihst,tihd->sihd', weights.astype(jnp.float32), col_v.astype(jnp.float32)).reshape(SEQUENCE_COUNT, RESIDUE_COUNT, CM)
    col_gated = (col_o * col_gate).astype(jnp.bfloat16)
    downward_change = jnp.dot(col_gated.reshape(SEQUENCE_COUNT * RESIDUE_COUNT, CM), vertical_result_matrix, preferred_element_type=jnp.float32).reshape(SEQUENCE_COUNT, RESIDUE_COUNT, CM) + vertical_result_shift
    post_downward_pass = (homology_table_refreshed.astype(jnp.float32) + downward_change).astype(jnp.bfloat16)
    trans_norm = normalize_lanes(post_downward_pass, feedforward_scaling_factor).astype(jnp.bfloat16)
    hidden = jax.nn.relu(jnp.dot(trans_norm.reshape(SEQUENCE_COUNT * RESIDUE_COUNT, CM), feedforward_expand_matrix, preferred_element_type=jnp.float32)).astype(jnp.bfloat16)
    trans_upd = jnp.dot(hidden, feedforward_shrink_matrix, preferred_element_type=jnp.float32).reshape(SEQUENCE_COUNT, RESIDUE_COUNT, CM)
    return (post_downward_pass.astype(jnp.float32) + trans_upd).astype(jnp.bfloat16)
```

```python
import functools
import math

import jax
import jax.numpy as jnp
from jax import lax
from jax.experimental import pallas as pl
from jax.experimental.pallas import tpu as pltpu
from jax.sharding import PartitionSpec as P

F32 = jnp.float32
BF16 = jnp.bfloat16
EPS = 1e-05
LOG2E = 1.4426950408889634
LANES = 128
MASK_LANE = 96
ONE_LANE = 97
MASKED = -1e30
VMEM = 56 * 2**20


def dot(a, b):
    return jnp.dot(a, b, preferred_element_type=F32)


def dot_nt(a, b):
    return lax.dot_general(a, b, (((1,), (1,)), ((), ())), preferred_element_type=F32)


def dot_tn(a, b):
    return lax.dot_general(a, b, (((0,), (0,)), ((), ())), preferred_element_type=F32)


def normalize(values, gain):
    center = values - jnp.mean(values, axis=-1, keepdims=True)
    spread = jnp.mean(center * center, axis=-1, keepdims=True)
    return center * lax.rsqrt(spread + EPS) * gain


def lanes_of(shape):
    return lax.broadcasted_iota(jnp.int32, shape, len(shape) - 1)


def pair_kernel(pair_ref, project_ref, bias_ref, rows_ref, *, channels, heads):
    for i in range(pair_ref.shape[0]):
        both = dot_nt(project_ref[...], pair_ref[i])
        center = both[:channels]
        spread = jnp.sum(center * center, axis=0, keepdims=True) * (1.0 / channels)
        raw = both[channels : channels + heads] + both[channels + heads :]
        rows_ref[:, i, :] = raw * lax.rsqrt(spread + EPS)
    bias_ref[...] = rows_ref[...].astype(BF16)


def pair_bias(coupled, gain, head_matrix, step):
    rows, cols, channels = coupled.shape
    heads = head_matrix.shape[1]
    gained = gain[:, None] * head_matrix.astype(F32) * LOG2E
    gained = (gained - jnp.mean(gained, axis=0, keepdims=True)).T
    high = gained.astype(BF16)
    low = (gained - high.astype(F32)).astype(BF16)
    centering = (jnp.eye(channels, dtype=F32) - 1.0 / channels).astype(BF16)
    project = jnp.concatenate([centering, high, low], axis=0)
    return pl.pallas_call(
        functools.partial(pair_kernel, channels=channels, heads=heads),
        grid=(rows // step,),
        in_specs=[
            pl.BlockSpec((step, cols, channels), lambda i: (i, 0, 0)),
            pl.BlockSpec(project.shape, lambda i: (0, 0)),
        ],
        out_specs=pl.BlockSpec((heads, step, cols), lambda i: (0, i, 0)),
        out_shape=jax.ShapeDtypeStruct((heads, rows, cols), BF16),
        scratch_shapes=[pltpu.VMEM((heads, step, cols), F32)],
        compiler_params=pltpu.CompilerParams(vmem_limit_bytes=VMEM),
        name="pair_bias",
    )(coupled, project)


def pack_kernel(table_ref, mask_ref, gain_ref, weight_ref, packed_ref, *, heads, scale):
    head_size = table_ref.shape[-1] // heads
    normed = normalize(table_ref[0].astype(F32), gain_ref[...]).astype(BF16)
    flat = dot(normed, weight_ref[...])
    lane = lanes_of((flat.shape[0], LANES))
    factor = jnp.where(lane < head_size, scale, 1.0)
    extra = jnp.where(
        lane == MASK_LANE, mask_ref[0], jnp.where(lane == ONE_LANE, 1.0, 0.0)
    )
    for h in range(heads):
        packed_ref[h, 0] = (flat[:, h * LANES : (h + 1) * LANES] * factor + extra).astype(BF16)


def pack_heads(table, mask, gain, weight, heads, scale):
    lines, residues, channels = table.shape
    head_size = channels // heads
    parts = weight.reshape(channels, 4, heads, head_size)
    parts = jnp.transpose(parts, (0, 2, 1, 3))
    parts = jnp.where(jnp.arange(4)[None, None, :, None] < 3, parts, 0)
    parts = parts.reshape(channels, heads * 4 * head_size)
    return pl.pallas_call(
        functools.partial(pack_kernel, heads=heads, scale=scale),
        grid=(lines,),
        in_specs=[
            pl.BlockSpec((1, residues, channels), lambda s: (s, 0, 0)),
            pl.BlockSpec((1, residues, 1), lambda s: (s, 0, 0)),
            pl.BlockSpec((1, channels), lambda s: (0, 0)),
            pl.BlockSpec(parts.shape, lambda s: (0, 0)),
        ],
        out_specs=pl.BlockSpec((heads, 1, residues, LANES), lambda s: (0, s, 0, 0)),
        out_shape=jax.ShapeDtypeStruct((heads, lines, residues, LANES), BF16),
        compiler_params=pltpu.CompilerParams(vmem_limit_bytes=VMEM),
        name="pack_heads",
    )(table, mask[:, :, None], gain[None, :], parts)


def row_kernel(own_ref, other_ref, bias_ref, out_ref, bias32_ref, score_ref, weight_ref, *, per, head_size, tile, chunk):
    blocks, lines, residues, _ = own_ref.shape
    queries = per * residues
    half = blocks * residues
    pieces = out_ref.shape[0]
    span = residues // pieces
    group = LANES // head_size
    for b in range(per):
        bias32_ref[b * residues : (b + 1) * residues] = bias_ref[b].astype(F32)
    lane = lanes_of((queries, LANES))
    first = pl.program_id(0) * per
    for pack in range(lines // group):
        total = jnp.zeros((queries, LANES), F32)
        for member in range(group):
            s = pack * group + member
            raw = jnp.concatenate([own_ref[first + b, s] for b in range(per)], axis=0)
            moved = pltpu.roll(raw.astype(F32), head_size, 1)
            query = jnp.where(
                (lane >= head_size) & (lane < 2 * head_size),
                moved,
                jnp.where(lane == MASK_LANE, 1.0, 0.0),
            ).astype(BF16)
            sources = [r[:, s].reshape(half, LANES) for r in (own_ref, other_ref)]
            for k in range(0, 2 * half, chunk):
                keys = sources[k // half][k % half : k % half + chunk]
                score_ref[:, k : k + chunk] = dot_nt(query, keys) + bias32_ref[:, k : k + chunk]
            for q in range(0, queries, tile):
                scores = score_ref[q : q + tile, :]
                top = jnp.max(scores, axis=1, keepdims=True)
                weight_ref[q : q + tile, :] = jnp.exp2(scores - top).astype(BF16)
            mixed = dot(weight_ref[:, :half], sources[0]) + dot(weight_ref[:, half:], sources[1])
            mixed = mixed / mixed[:, ONE_LANE : ONE_LANE + 1]
            mixed = pltpu.roll(mixed, (member * head_size - 2 * head_size) % LANES, 1)
            here = (lane >= member * head_size) & (lane < (member + 1) * head_size)
            total = jnp.where(here, mixed, total)
        for b in range(per):
            for piece in range(pieces):
                start = b * residues + piece * span
                out_ref[piece, b, pack * span : (pack + 1) * span, :] = total[start : start + span].astype(BF16)


def row_attention(own, other, bias, pieces, head_size, per):
    blocks, lines, residues, _ = own.shape
    queries = per * residues
    keys = 2 * blocks * residues
    rows = lines * head_size // LANES * residues // pieces
    whole = pl.BlockSpec(own.shape, lambda i: (0, 0, 0, 0))
    return pl.pallas_call(
        functools.partial(row_kernel, per=per, head_size=head_size, tile=16, chunk=256),
        grid=(blocks // per,),
        in_specs=[
            whole,
            whole,
            pl.BlockSpec((per, residues, keys), lambda i: (i, 0, 0)),
        ],
        out_specs=pl.BlockSpec((pieces, per, rows, LANES), lambda i: (0, i, 0, 0)),
        out_shape=jax.ShapeDtypeStruct((pieces, blocks, rows, LANES), BF16),
        scratch_shapes=[
            pltpu.VMEM((queries, keys), F32),
            pltpu.VMEM((queries, keys), F32),
            pltpu.VMEM((queries, keys), BF16),
        ],
        compiler_params=pltpu.CompilerParams(vmem_limit_bytes=VMEM),
        name="row_attention",
    )(own, other, bias)


def column_kernel(
    mixed_ref, table_ref, mask_ref,
    row_gain_ref, row_gate_ref, row_shift_ref, row_out_ref, row_bias_ref,
    col_gain_ref, col_weight_ref, col_shift_ref, col_out_ref, col_bias_ref,
    ff_gain_ref, expand_ref, shrink_ref, out_ref, *, heads, scale,
):
    groups, span, lines, channels = table_ref.shape
    rows = groups * lines
    head_size = channels // heads
    table = table_ref[...].astype(F32)
    table = jnp.concatenate([table[:, i].reshape(rows, channels) for i in range(span)], axis=0)
    mixed = mixed_ref[...].reshape(span * rows, channels).astype(F32)

    row_in = normalize(table, row_gain_ref[...]).astype(BF16)
    gate = jax.nn.sigmoid(dot(row_in, row_gate_ref[...]) + row_shift_ref[...])
    gated = (mixed * gate).astype(BF16)
    after_rows = table + (dot(gated, row_out_ref[...]) + row_bias_ref[...])
    after_rows = after_rows.astype(BF16).astype(F32)

    col_in = normalize(after_rows, col_gain_ref[...]).astype(BF16)
    projected = dot(col_in, col_weight_ref[...])
    query = (projected[:, :channels] * scale).astype(BF16)
    key = projected[:, channels : 2 * channels].astype(BF16)
    value = projected[:, 2 * channels : 3 * channels].astype(BF16)
    gate = jax.nn.sigmoid(projected[:, 3 * channels :] + col_shift_ref[...])

    shape = (heads * rows, channels)
    row_head = lax.broadcasted_iota(jnp.int32, shape, 0) // rows
    same = row_head == lax.broadcasted_iota(jnp.int32, shape, 1) // head_size
    same = jnp.where(same, 1.0, 0.0).astype(BF16)
    masks = mask_ref[:, 0].astype(F32).reshape(rows, channels)
    mask_lane = lanes_of((rows, channels))
    attended = []
    for i in range(span):
        here = slice(i * rows, (i + 1) * rows)
        spread_key = jnp.concatenate([key[here]] * heads, axis=0) * same
        spread_value = jnp.concatenate([value[here]] * heads, axis=0) * same
        scores = dot_nt(spread_key, query[here]).reshape(heads, rows, rows)
        place = pl.program_id(0) * span + i
        present = jnp.sum(jnp.where(mask_lane == place, masks, 0.0), axis=1, keepdims=True)
        scores = jnp.where(present[None] > 0, scores, -1e9)
        top = jnp.max(scores, axis=1, keepdims=True)
        weights = jnp.exp2(scores - top)
        weights = weights / jnp.sum(weights, axis=1, keepdims=True)
        weights = weights.astype(BF16).reshape(heads * rows, rows)
        attended.append(dot_tn(weights, spread_value))
    gated = (jnp.concatenate(attended, axis=0) * gate).astype(BF16)
    after_cols = after_rows + (dot(gated, col_out_ref[...]) + col_bias_ref[...])
    after_cols = after_cols.astype(BF16).astype(F32)

    trans_in = normalize(after_cols, ff_gain_ref[...]).astype(BF16)
    hidden = jnp.maximum(dot(trans_in, expand_ref[...]), 0.0).astype(BF16)
    updated = after_cols + dot(hidden, shrink_ref[...])
    for i in range(span):
        block = updated[i * rows : (i + 1) * rows].reshape(groups, lines, channels)
        out_ref[:, i] = block.astype(BF16)


def column_phase(mixed, table, params, heads, scale, span):
    groups, extended, lines, channels = table.shape
    residues = extended - 1
    token_block = pl.BlockSpec((groups, span, lines, channels), lambda i: (0, i, 0, 0))
    in_specs = [
        pl.BlockSpec((span, groups * lines, channels), lambda i: (i, 0, 0)),
        token_block,
        pl.BlockSpec((groups, 1, lines, channels), lambda i: (0, residues, 0, 0)),
    ]
    in_specs += [pl.BlockSpec(p.shape, lambda i: (0, 0)) for p in params]
    return pl.pallas_call(
        functools.partial(column_kernel, heads=heads, scale=scale),
        grid=(residues // span,),
        in_specs=in_specs,
        out_specs=token_block,
        out_shape=jax.ShapeDtypeStruct((groups, residues, lines, channels), BF16),
        compiler_params=pltpu.CompilerParams(vmem_limit_bytes=VMEM),
        name="column_phase",
    )(mixed, table, table, *params)


def shards(
    seq_size,
    res_size,
    homology_table,
    coupled_state,
    aligned_indicator,
    amino_indicator,
    horizontal_scaling_factor,
    horizontal_projection_matrix,
    horizontal_sigmoid_shift,
    horizontal_result_matrix,
    horizontal_result_shift,
    coupling_scaling_factor,
    coupling_head_matrix,
    downward_stretch_vector,
    vertical_projection_matrix,
    vertical_sigmoid_shift,
    vertical_result_matrix,
    vertical_result_shift,
    feedforward_scaling_factor,
    feedforward_expand_matrix,
    feedforward_shrink_matrix,
):
    lines, residues, channels = homology_table.shape
    heads = coupling_head_matrix.shape[1]
    head_size = channels // heads
    scale = LOG2E / math.sqrt(head_size)
    span = residues // seq_size
    core = lax.axis_index("res") % 2
    parity = [list(range(p, res_size, 2)) for p in (0, 1)]
    parity_all = [[r * res_size + c for r in range(seq_size) for c in group] for group in parity]

    by_residue = jnp.transpose(homology_table, (1, 0, 2)).reshape(seq_size, span, lines, channels)
    mask_row = jnp.transpose(aligned_indicator.reshape(lines, seq_size, span), (1, 0, 2))
    mask_row = jnp.pad(mask_row.astype(BF16), ((0, 0), (0, 0), (0, channels - span)))
    columns = jnp.concatenate([by_residue, mask_row[:, None]], axis=1)
    columns = lax.all_to_all(columns, "seq", 0, 0)

    tile_bias = pair_bias(coupled_state, coupling_scaling_factor, coupling_head_matrix, 32)
    rows = tile_bias.shape[1] // 2
    sent = lax.all_to_all(tile_bias.reshape(res_size, rows, residues), "res", 0, 0)
    sent = sent.reshape(res_size // 2, 2, rows, residues)
    near = lax.dynamic_index_in_dim(sent, core, 1, keepdims=True)
    far = lax.dynamic_index_in_dim(sent, 1 - core, 1, keepdims=True)
    row_bias = jnp.transpose(jnp.concatenate([near, far], axis=1), (2, 1, 0, 3))
    row_bias = row_bias.reshape(rows, res_size * residues)
    bias = lax.all_gather(row_bias, "seq", axis=0)

    present = aligned_indicator * amino_indicator[None, :]
    mask = jnp.where(present > 0, 0.0, MASKED).astype(F32)
    packed = pack_heads(
        homology_table, mask, horizontal_scaling_factor, horizontal_projection_matrix, heads, scale
    )
    own = lax.all_to_all(packed, "res", 0, 0, axis_index_groups=parity)
    other = lax.ppermute(own, "res", [(c, c ^ 1) for c in range(res_size)])

    mixed = row_attention(own, other, bias, seq_size, head_size, 2)
    mixed = mixed.reshape((seq_size * res_size // 2,) + mixed.shape[2:])
    mixed = lax.all_to_all(mixed, ("seq", "res"), 0, 0, axis_index_groups=parity_all)
    group = LANES // head_size
    mixed = mixed.reshape(seq_size, heads, lines // group, span, group, head_size)
    mixed = jnp.transpose(mixed, (3, 0, 2, 4, 1, 5)).reshape(span, seq_size * lines, channels)

    params = [
        horizontal_scaling_factor[None],
        horizontal_projection_matrix[:, 3 * channels :],
        horizontal_sigmoid_shift[None],
        horizontal_result_matrix,
        horizontal_result_shift[None],
        downward_stretch_vector[None],
        vertical_projection_matrix,
        vertical_sigmoid_shift[None],
        vertical_result_matrix,
        vertical_result_shift[None],
        feedforward_scaling_factor[None],
        feedforward_expand_matrix,
        feedforward_shrink_matrix,
    ]
    updated = column_phase(mixed, columns, params, heads, scale, 4)
    updated = lax.all_to_all(updated, "seq", 0, 0)
    return jnp.transpose(updated.reshape(residues, lines, channels), (1, 0, 2))


def solution(mesh):
    table = P("seq", "res", None)
    return jax.shard_map(
        functools.partial(shards, mesh.shape["seq"], mesh.shape["res"]),
        mesh=mesh,
        in_specs=(table, table, P("seq", "res"), P("res")) + (P(),) * 15,
        out_specs=table,
        check_vma=False,
    )
```

```python
import functools
import math

import jax
import jax.numpy as jnp
from jax import lax
from jax.experimental import pallas as pl
from jax.experimental.pallas import tpu as pltpu
from jax.sharding import PartitionSpec as P

F32 = jnp.float32
BF16 = jnp.bfloat16
EPS = 1e-05
LOG2E = 1.4426950408889634
LANES = 128
MASK_LANE = 96
ONE_LANE = 97
MASKED = -1e30
VMEM = 56 * 2**20


def dot(a, b):
    return jnp.dot(a, b, preferred_element_type=F32)


def dot_nt(a, b):
    return lax.dot_general(a, b, (((1,), (1,)), ((), ())), preferred_element_type=F32)


def dot_tn(a, b):
    return lax.dot_general(a, b, (((0,), (0,)), ((), ())), preferred_element_type=F32)


def normalize(values, gain):
    center = values - jnp.mean(values, axis=-1, keepdims=True)
    spread = jnp.mean(center * center, axis=-1, keepdims=True)
    return center * lax.rsqrt(spread + EPS) * gain


def lanes_of(shape):
    return lax.broadcasted_iota(jnp.int32, shape, len(shape) - 1)


STEP = 32
GROUPS = 4
EIGHT = 8
STEP_ROWS = STEP + EIGHT


def pair_kernel(pair_ref, gain_ref, head_ref, bias_ref, project_ref, rows_ref):
    channels, heads = head_ref.shape

    @pl.when(pl.program_id(0) == 0)
    def _():
        gained = (gain_ref[...] * LOG2E) * head_ref[...].astype(F32).T
        gained = gained - jnp.mean(gained, axis=1, keepdims=True)
        high = gained.astype(BF16)
        low = (gained - high.astype(F32)).astype(BF16)
        same = lax.broadcasted_iota(jnp.int32, (channels, channels), 0) == lanes_of((channels, channels))
        centering = jnp.where(same, 1.0, 0.0) - 1.0 / channels
        project_ref[:channels] = centering.astype(BF16)
        project_ref[channels:] = jnp.concatenate([high.astype(F32), low.astype(F32)], axis=0).astype(BF16)

    def project(tokens):
        both = dot_nt(project_ref[...], tokens)
        center = both[:channels]
        spread = jnp.sum(center * center, axis=0, keepdims=True) * (1.0 / channels)
        raw = both[channels : channels + heads] + both[channels + heads :]
        return raw * lax.rsqrt(spread + EPS)

    for i in range(0, STEP, 2):
        done = project(pair_ref[i : i + 2, :LANES, :].reshape(2 * LANES, channels))
        rows_ref[:, i, :] = done[:, :LANES]
        rows_ref[:, i + 1, :] = done[:, LANES:]
    for r in range(0, EIGHT, 2):
        rest = [pair_ref[g * EIGHT + r + e, LANES:, :] for e in range(2) for g in range(GROUPS)]
        done = project(jnp.concatenate(rest, axis=0))
        rows_ref[:, STEP + r, :] = done[:, :LANES]
        rows_ref[:, STEP + r + 1, :] = done[:, LANES:]
    bias_ref[:, 0] = rows_ref[...].astype(BF16)


def pair_bias(coupled, gain, head_matrix):
    rows, cols, channels = coupled.shape
    heads = head_matrix.shape[1]
    return pl.pallas_call(
        pair_kernel,
        grid=(rows // STEP,),
        in_specs=[
            pl.BlockSpec((STEP, cols, channels), lambda i: (i, 0, 0)),
            pl.BlockSpec((1, channels), lambda i: (0, 0)),
            pl.BlockSpec((channels, heads), lambda i: (0, 0)),
        ],
        out_specs=pl.BlockSpec((heads, 1, STEP_ROWS, LANES), lambda i: (0, i, 0, 0)),
        out_shape=jax.ShapeDtypeStruct((heads, rows // STEP, STEP_ROWS, LANES), BF16),
        scratch_shapes=[
            pltpu.VMEM((channels + 2 * heads, channels), BF16),
            pltpu.VMEM((heads, STEP_ROWS, LANES), F32),
        ],
        compiler_params=pltpu.CompilerParams(vmem_limit_bytes=VMEM),
        name="pair_bias",
    )(coupled, gain[None], head_matrix)


def pack_kernel(table_ref, mask_ref, gain_ref, weight_ref, packed_ref, *, heads, scale):
    head_size = table_ref.shape[-1] // heads
    normed = normalize(table_ref[0].astype(F32), gain_ref[...]).astype(BF16)
    flat = dot(normed, weight_ref[...])
    lane = lanes_of((flat.shape[0], LANES))
    factor = jnp.where(lane < head_size, scale, 1.0)
    extra = jnp.where(
        lane == MASK_LANE, mask_ref[0], jnp.where(lane == ONE_LANE, 1.0, 0.0)
    )
    for h in range(heads):
        packed_ref[h, 0] = (flat[:, h * LANES : (h + 1) * LANES] * factor + extra).astype(BF16)


def pack_heads(table, mask, gain, weight, heads, scale):
    lines, residues, channels = table.shape
    head_size = channels // heads
    parts = weight.reshape(channels, 4, heads, head_size)
    parts = jnp.transpose(parts, (0, 2, 1, 3))
    parts = jnp.where(jnp.arange(4)[None, None, :, None] < 3, parts, 0)
    parts = parts.reshape(channels, heads * 4 * head_size)
    return pl.pallas_call(
        functools.partial(pack_kernel, heads=heads, scale=scale),
        grid=(lines,),
        in_specs=[
            pl.BlockSpec((1, residues, channels), lambda s: (s, 0, 0)),
            pl.BlockSpec((1, residues, 1), lambda s: (s, 0, 0)),
            pl.BlockSpec((1, channels), lambda s: (0, 0)),
            pl.BlockSpec(parts.shape, lambda s: (0, 0)),
        ],
        out_specs=pl.BlockSpec((heads, 1, residues, LANES), lambda s: (0, s, 0, 0)),
        out_shape=jax.ShapeDtypeStruct((heads, lines, residues, LANES), BF16),
        compiler_params=pltpu.CompilerParams(vmem_limit_bytes=VMEM),
        name="pack_heads",
    )(table, mask[:, :, None], gain[None, :], parts)


TILE = 16


def row_kernel(place_ref, own_ref, other_ref, *rest, parts, head_size):
    count = sum(parts)
    bias_refs, (out_ref, bias32_ref, score_ref, weight_ref) = rest[:count], rest[count:]
    blocks, lines, residues, _ = own_ref.shape
    pairs, queries, keys = bias32_ref.shape
    per = queries // residues
    pieces = out_ref.shape[0]
    span = residues // pieces
    group = LANES // head_size
    chunk = 2 * LANES
    core = place_ref[0]
    lane8 = lanes_of((EIGHT, LANES))
    lane = lanes_of((queries, LANES))

    at = 0
    for block, number in enumerate(parts):
        refs = bias_refs[at : at + number]
        at += number
        pair, row0 = block // per, (block % per) * residues
        for side in range(2):
            parity = core if side == 0 else 1 - core
            for step in range(residues // STEP):
                row = row0 + step * STEP
                tails = []
                for k in range(blocks):
                    each = blocks // number
                    tile = refs[k // each][2 * (k % each) + parity, step].astype(F32)
                    column = (side * blocks + k) * LANES
                    bias32_ref[pair, row : row + STEP, column : column + LANES] = tile[:STEP]
                    tails.append(tile[STEP:])
                for q in range(blocks // GROUPS):
                    column = 2 * blocks * LANES + (side * blocks // GROUPS + q) * LANES
                    for g in range(GROUPS):
                        total = None
                        for e in range(GROUPS):
                            moved = tails[q * GROUPS + e]
                            if e != g:
                                moved = pltpu.roll(moved, ((e - g) * STEP) % LANES, 1)
                            total = moved if total is None else jnp.where(lane8 >= e * STEP, moved, total)
                        bias32_ref[pair, row + g * EIGHT : row + (g + 1) * EIGHT, column : column + LANES] = total

    def key_chunk(s, j):
        each = blocks // 2
        if j < 2 * each:
            ref = own_ref if j < each else other_ref
            k = 2 * (j % each)
            return ref[k : k + 2, s, :LANES, :].reshape(chunk, LANES)
        ref = own_ref if j == 2 * each else other_ref
        return ref[:, s, LANES:, :].reshape(chunk, LANES)

    def both_of(s):
        first = [r[:, s, :LANES, :].reshape(blocks * LANES, LANES) for r in (own_ref, other_ref)]
        last = [r[:, s, LANES:, :].reshape(chunk, LANES) for r in (own_ref, other_ref)]
        return first + last

    def body(pair, carry):
        for pack in range(lines // group):
            total = jnp.zeros((queries, LANES), F32)
            for member in range(group):
                s = pack * group + member
                raw = [own_ref[place_ref[1 + pair * per + b], s] for b in range(per)]
                moved = pltpu.roll(jnp.concatenate(raw, axis=0).astype(F32), head_size, 1)
                inside = (lane >= head_size) & (lane < 2 * head_size)
                query = jnp.where(inside, moved, jnp.where(lane == MASK_LANE, 1.0, 0.0)).astype(BF16)
                for j in range(keys // chunk):
                    columns = slice(j * chunk, (j + 1) * chunk)
                    score_ref[:, columns] = dot_nt(query, key_chunk(s, j)) + bias32_ref[pair, :, columns]
                for q in range(0, queries, TILE):
                    scores = score_ref[q : q + TILE, :]
                    top = jnp.max(scores, axis=1, keepdims=True)
                    weight_ref[q : q + TILE, :] = jnp.exp2(scores - top).astype(BF16)
                mixed, column = None, 0
                for values in both_of(s):
                    product = dot(weight_ref[:, column : column + values.shape[0]], values)
                    column += values.shape[0]
                    mixed = product if mixed is None else mixed + product
                mixed = mixed / mixed[:, ONE_LANE : ONE_LANE + 1]
                mixed = pltpu.roll(mixed, (member * head_size - 2 * head_size) % LANES, 1)
                here = (lane >= member * head_size) & (lane < (member + 1) * head_size)
                total = jnp.where(here, mixed, total)
            for b in range(per):
                target = place_ref[1 + pair * per + b] % len(parts)
                for piece in range(pieces):
                    row = b * residues + piece * span
                    out_ref[piece, target, pack * span : (pack + 1) * span, :] = total[row : row + span].astype(BF16)
        return carry

    lax.fori_loop(0, pairs, body, 0)


def row_attention(place, own, other, biases, pieces, head_size, per):
    blocks, lines, residues, _ = own.shape
    queries = per * residues
    keys = 2 * blocks * residues
    packs = lines * head_size // LANES
    parts = tuple(len(b) for b in biases)
    flat = [b for several in biases for b in several]
    pairs = len(parts) // per
    rows = packs * residues // pieces
    scores = lines * len(parts) * residues * keys
    return pl.pallas_call(
        functools.partial(row_kernel, parts=parts, head_size=head_size),
        in_specs=[pl.BlockSpec(memory_space=pltpu.SMEM)]
        + [pl.BlockSpec(memory_space=pltpu.VMEM)] * (2 + len(flat)),
        out_specs=pl.BlockSpec(memory_space=pltpu.VMEM),
        out_shape=jax.ShapeDtypeStruct((pieces, len(parts), rows, LANES), BF16),
        scratch_shapes=[
            pltpu.VMEM((pairs, queries, keys), F32),
            pltpu.VMEM((queries, keys), F32),
            pltpu.VMEM((queries, keys), BF16),
        ],
        compiler_params=pltpu.CompilerParams(vmem_limit_bytes=VMEM),
        cost_estimate=pl.CostEstimate(flops=scores * 512, bytes_accessed=12_000_000, transcendentals=scores),
        name="row_attention",
    )(place, own, other, *flat)


def column_kernel(
    mixed_ref, table_ref, mask_ref,
    row_gain_ref, row_gate_ref, row_shift_ref, row_out_ref, row_bias_ref,
    col_gain_ref, col_weight_ref, col_shift_ref, col_out_ref, col_bias_ref,
    ff_gain_ref, expand_ref, shrink_ref, out_ref, mixed32_ref, *, heads, scale,
):
    groups, span, lines, channels = table_ref.shape
    rows = groups * lines
    head_size = channels // heads

    @pl.when(pl.program_id(0) == 0)
    def _():
        members = LANES // head_size
        packs = lines // members
        received = mixed_ref.shape[2]
        residues = received // packs
        source = lax.broadcasted_iota(jnp.int32, (LANES, channels), 0)
        target = lanes_of((LANES, channels))
        tokens = [mixed_ref[:, h].astype(F32).reshape(groups * received, LANES).astype(BF16) for h in range(heads)]
        for member in range(members):
            total = None
            for h in range(heads):
                move = (target // head_size == h) & (source == target - h * head_size + member * head_size)
                part = dot(tokens[h], jnp.where(move, 1.0, 0.0).astype(BF16))
                total = part if total is None else total + part
            for r in range(groups):
                for pack in range(packs):
                    row = r * received + pack * residues
                    line = r * lines + pack * members + member
                    for part in range(channels // LANES):
                        mixed32_ref[part, pl.ds(line, residues, stride=rows), :] = total[
                            row : row + residues, part * LANES : (part + 1) * LANES
                        ]

    table = table_ref[...].astype(F32)
    table = jnp.concatenate([table[:, i].reshape(rows, channels) for i in range(span)], axis=0)
    here = pl.ds(pl.program_id(0) * span * rows, span * rows)
    mixed = jnp.concatenate([mixed32_ref[part, here, :] for part in range(channels // LANES)], axis=1)

    row_in = normalize(table, row_gain_ref[...]).astype(BF16)
    gate = jax.nn.sigmoid(dot(row_in, row_gate_ref[...]) + row_shift_ref[...])
    gated = (mixed * gate).astype(BF16)
    after_rows = table + (dot(gated, row_out_ref[...]) + row_bias_ref[...])
    after_rows = after_rows.astype(BF16).astype(F32)

    col_in = normalize(after_rows, col_gain_ref[...]).astype(BF16)
    projected = dot(col_in, col_weight_ref[...])
    query = (projected[:, :channels] * scale).astype(BF16)
    key = projected[:, channels : 2 * channels].astype(BF16)
    value = projected[:, 2 * channels : 3 * channels].astype(BF16)
    gate = jax.nn.sigmoid(projected[:, 3 * channels :] + col_shift_ref[...])

    shape = (heads * rows, channels)
    row_head = lax.broadcasted_iota(jnp.int32, shape, 0) // rows
    same = row_head == lax.broadcasted_iota(jnp.int32, shape, 1) // head_size
    same = jnp.where(same, 1.0, 0.0).astype(BF16)
    masks = mask_ref[:, 0].astype(F32).reshape(rows, channels)
    mask_lane = lanes_of((rows, channels))
    attended = []
    for i in range(span):
        here = slice(i * rows, (i + 1) * rows)
        spread_key = jnp.concatenate([key[here]] * heads, axis=0) * same
        spread_value = jnp.concatenate([value[here]] * heads, axis=0) * same
        scores = dot_nt(spread_key, query[here]).reshape(heads, rows, rows)
        place = pl.program_id(0) * span + i
        present = jnp.sum(jnp.where(mask_lane == place, masks, 0.0), axis=1, keepdims=True)
        scores = jnp.where(present[None] > 0, scores, -1e9)
        top = jnp.max(scores, axis=1, keepdims=True)
        weights = jnp.exp2(scores - top)
        weights = weights / jnp.sum(weights, axis=1, keepdims=True)
        weights = weights.astype(BF16).reshape(heads * rows, rows)
        attended.append(dot_tn(weights, spread_value))
    gated = (jnp.concatenate(attended, axis=0) * gate).astype(BF16)
    after_cols = after_rows + (dot(gated, col_out_ref[...]) + col_bias_ref[...])
    after_cols = after_cols.astype(BF16).astype(F32)

    trans_in = normalize(after_cols, ff_gain_ref[...]).astype(BF16)
    hidden = jnp.maximum(dot(trans_in, expand_ref[...]), 0.0).astype(BF16)
    updated = after_cols + dot(hidden, shrink_ref[...])
    for i in range(span):
        block = updated[i * rows : (i + 1) * rows].reshape(groups, lines, channels)
        out_ref[:, i] = block.astype(BF16)


def column_phase(mixed, table, params, heads, scale, span):
    groups, extended, lines, channels = table.shape
    residues = extended - 1
    token_block = pl.BlockSpec((groups, span, lines, channels), lambda i: (0, i, 0, 0))
    in_specs = [
        pl.BlockSpec(mixed.shape, lambda i: (0, 0, 0, 0)),
        token_block,
        pl.BlockSpec((groups, 1, lines, channels), lambda i: (0, residues, 0, 0)),
    ]
    in_specs += [pl.BlockSpec(p.shape, lambda i: (0, 0)) for p in params]
    return pl.pallas_call(
        functools.partial(column_kernel, heads=heads, scale=scale),
        grid=(residues // span,),
        in_specs=in_specs,
        out_specs=token_block,
        out_shape=jax.ShapeDtypeStruct((groups, residues, lines, channels), BF16),
        scratch_shapes=[pltpu.VMEM((channels // LANES, residues * groups * lines, LANES), F32)],
        compiler_params=pltpu.CompilerParams(vmem_limit_bytes=VMEM),
        name="column_phase",
    )(mixed, table, table, *params)


def shards(
    seq_size,
    res_size,
    homology_table,
    coupled_state,
    aligned_indicator,
    amino_indicator,
    horizontal_scaling_factor,
    horizontal_projection_matrix,
    horizontal_sigmoid_shift,
    horizontal_result_matrix,
    horizontal_result_shift,
    coupling_scaling_factor,
    coupling_head_matrix,
    downward_stretch_vector,
    vertical_projection_matrix,
    vertical_sigmoid_shift,
    vertical_result_matrix,
    vertical_result_shift,
    feedforward_scaling_factor,
    feedforward_expand_matrix,
    feedforward_shrink_matrix,
):
    lines, residues, channels = homology_table.shape
    heads = coupling_head_matrix.shape[1]
    head_size = channels // heads
    scale = LOG2E / math.sqrt(head_size)
    span = residues // seq_size
    core = lax.axis_index("res") % 2
    parity = [list(range(p, res_size, 2)) for p in (0, 1)]
    parity_all = [[r * res_size + c for r in range(seq_size) for c in group] for group in parity]

    tile_bias = pair_bias(coupled_state, coupling_scaling_factor, coupling_head_matrix)
    tile_bias, homology_table = lax.optimization_barrier((tile_bias, homology_table))
    steps = tile_bias.shape[1] // 2
    near = lax.all_to_all(tile_bias.reshape(res_size, steps, STEP_ROWS, LANES), "res", 0, 0)

    by_residue = jnp.transpose(homology_table, (1, 0, 2)).reshape(seq_size, span, lines, channels)
    mask_row = jnp.transpose(aligned_indicator.reshape(lines, seq_size, span), (1, 0, 2))
    mask_row = jnp.pad(mask_row.astype(BF16), ((0, 0), (0, 0), (0, channels - span)))
    columns = jnp.concatenate([by_residue, mask_row[:, None]], axis=1)

    present = aligned_indicator * amino_indicator[None, :]
    mask = jnp.where(present > 0, 0.0, MASKED).astype(F32)
    packed = pack_heads(
        homology_table, mask, horizontal_scaling_factor, horizontal_projection_matrix, heads, scale
    )
    near, packed, columns = lax.optimization_barrier((near, packed, columns))
    own = lax.all_to_all(packed, "res", 0, 0, axis_index_groups=parity)

    ring = seq_size // 2

    def around(values, by):
        return lax.ppermute(
            values, "seq", [(h * ring + z, h * ring + (z + by) % ring) for h in (0, 1) for z in range(ring)]
        )

    def swap(values):
        return lax.ppermute(values, "seq", [(r, (r + ring) % seq_size) for r in range(seq_size)])

    middle = res_size // 2
    up, down, far = around(near, 1), around(near, -1), swap(near)
    across = [around(up[:middle], 1), around(down[middle:], -1)]
    own, up, down, far, across = lax.optimization_barrier((own, up, down, far, across))
    other = lax.ppermute(own, "res", [(c, c ^ 1) for c in range(res_size)])
    near_biases = [[near], [up], [down], across]
    far_biases = [[far], [around(far, 1)], [around(far, -1)], [swap(a) for a in across]]

    me = lax.axis_index("seq")
    half, z = me // ring, me % ring
    order = [0, -1, 1, 2]
    places = [
        jnp.stack([core] + [((half + turn) % 2) * ring + (z + o) % ring for o in order]).astype(jnp.int32)
        for turn in range(2)
    ]
    mixed = row_attention(places[0], own, other, near_biases, seq_size, head_size, 2)
    columns = lax.all_to_all(columns, "seq", 0, 0)
    place, mixed, columns = lax.optimization_barrier((places[1], mixed, columns))
    mixed = [mixed, row_attention(place, own, other, far_biases, seq_size, head_size, 2)]
    mixed = jnp.where(
        half == 0, jnp.concatenate(mixed, axis=1), jnp.concatenate(mixed[::-1], axis=1)
    )
    mixed = mixed.reshape((seq_size * ring * 2,) + mixed.shape[2:])
    mixed = lax.all_to_all(mixed, ("seq", "res"), 0, 0, axis_index_groups=parity_all)
    mixed = mixed.reshape((seq_size, heads) + mixed.shape[1:])

    params = [
        horizontal_scaling_factor[None],
        horizontal_projection_matrix[:, 3 * channels :],
        horizontal_sigmoid_shift[None],
        horizontal_result_matrix,
        horizontal_result_shift[None],
        downward_stretch_vector[None],
        vertical_projection_matrix,
        vertical_sigmoid_shift[None],
        vertical_result_matrix,
        vertical_result_shift[None],
        feedforward_scaling_factor[None],
        feedforward_expand_matrix,
        feedforward_shrink_matrix,
    ]
    updated = column_phase(mixed, columns, params, heads, scale, span)
    updated = lax.all_to_all(updated, "seq", 0, 0)
    return jnp.transpose(updated.reshape(residues, lines, channels), (1, 0, 2))


def solution(mesh):
    table = P("seq", "res", None)
    return jax.shard_map(
        functools.partial(shards, mesh.shape["seq"], mesh.shape["res"]),
        mesh=mesh,
        in_specs=(table, table, P("seq", "res"), P("res")) + (P(),) * 15,
        out_specs=table,
        check_vma=False,
    )
```

```python
import functools
import math

import jax
import jax.numpy as jnp
from jax import lax
from jax.experimental import pallas as pl
from jax.experimental.pallas import tpu as pltpu
from jax.sharding import PartitionSpec as P

F32 = jnp.float32
BF16 = jnp.bfloat16
EPS = 1e-05
LOG2E = 1.4426950408889634
LANES = 128
MASKED = -1e30
VMEM = 56 * 2**20
ROW_VMEM = 40 * 2**20


def dot(a, b):
    return jnp.dot(a, b, preferred_element_type=F32)


def dot_nt(a, b):
    return lax.dot_general(a, b, (((1,), (1,)), ((), ())), preferred_element_type=F32)


def dot_tn(a, b):
    return lax.dot_general(a, b, (((0,), (0,)), ((), ())), preferred_element_type=F32)


def normalize(values, gain):
    center = values - jnp.mean(values, axis=-1, keepdims=True)
    spread = jnp.mean(center * center, axis=-1, keepdims=True)
    return center * lax.rsqrt(spread + EPS) * gain


def lanes_of(shape):
    return lax.broadcasted_iota(jnp.int32, shape, len(shape) - 1)


STEP = 32
GROUPS = 4
EIGHT = 8
STEP_ROWS = STEP + EIGHT


def pair_kernel(pair_ref, gain_ref, head_ref, bias_ref, project_ref, rows_ref):
    channels, heads = head_ref.shape

    @pl.when(pl.program_id(0) == 0)
    def _():
        gained = (gain_ref[...] * LOG2E) * head_ref[...].astype(F32).T
        gained = gained - jnp.mean(gained, axis=1, keepdims=True)
        high = gained.astype(BF16)
        low = (gained - high.astype(F32)).astype(BF16)
        same = lax.broadcasted_iota(jnp.int32, (channels, channels), 0) == lanes_of((channels, channels))
        centering = jnp.where(same, 1.0, 0.0) - 1.0 / channels
        project_ref[:channels] = centering.astype(BF16)
        project_ref[channels:] = jnp.concatenate([high.astype(F32), low.astype(F32)], axis=0).astype(BF16)

    def project(tokens):
        both = dot_nt(project_ref[...], tokens)
        center = both[:channels]
        spread = jnp.sum(center * center, axis=0, keepdims=True) * (1.0 / channels)
        raw = both[channels : channels + heads] + both[channels + heads :]
        return raw * lax.rsqrt(spread + EPS)

    for i in range(0, STEP, 2):
        done = project(pair_ref[i : i + 2, :LANES, :].reshape(2 * LANES, channels))
        rows_ref[:, i, :] = done[:, :LANES]
        rows_ref[:, i + 1, :] = done[:, LANES:]
    for r in range(0, EIGHT, 2):
        rest = [pair_ref[g * EIGHT + r + e, LANES:, :] for e in range(2) for g in range(GROUPS)]
        done = project(jnp.concatenate(rest, axis=0))
        rows_ref[:, STEP + r, :] = done[:, :LANES]
        rows_ref[:, STEP + r + 1, :] = done[:, LANES:]
    bias_ref[:, 0] = rows_ref[...].astype(BF16)


def pair_bias(coupled, gain, head_matrix):
    rows, cols, channels = coupled.shape
    heads = head_matrix.shape[1]
    return pl.pallas_call(
        pair_kernel,
        grid=(rows // STEP,),
        in_specs=[
            pl.BlockSpec((STEP, cols, channels), lambda i: (i, 0, 0)),
            pl.BlockSpec((1, channels), lambda i: (0, 0)),
            pl.BlockSpec((channels, heads), lambda i: (0, 0)),
        ],
        out_specs=pl.BlockSpec((heads, 1, STEP_ROWS, LANES), lambda i: (0, i, 0, 0)),
        out_shape=jax.ShapeDtypeStruct((heads, rows // STEP, STEP_ROWS, LANES), BF16),
        scratch_shapes=[
            pltpu.VMEM((channels + 2 * heads, channels), BF16),
            pltpu.VMEM((heads, STEP_ROWS, LANES), F32),
        ],
        compiler_params=pltpu.CompilerParams(vmem_limit_bytes=VMEM),
        name="pair_bias",
    )(coupled, gain[None], head_matrix)


MASK_ROWS = 16


def pack_kernel(table_ref, mask_ref, gain_ref, weight_ref, packed_ref, *, scale):
    group, residues, channels = table_ref.shape
    heads = packed_ref.shape[0]
    head_size = channels // heads
    lane = lanes_of((residues, LANES))
    flat = []
    for member in range(group):
        normed = normalize(table_ref[member].astype(F32), gain_ref[...]).astype(BF16)
        flat.append(dot(normed, weight_ref[:, : 3 * channels]))
    for h in range(heads):
        for kind in range(3):
            column = kind * channels + h // group * LANES
            total = None
            for member in range(group):
                part = flat[member][:, column : column + LANES]
                if member != h % group:
                    part = pltpu.roll(part, ((member - h % group) * head_size) % LANES, 1)
                total = part if total is None else jnp.where(lane >= member * head_size, part, total)
            if kind == 0:
                total = total * scale
            packed_ref[h, 0, kind * residues : (kind + 1) * residues] = total.astype(BF16)
        packed_ref[h, 0, 3 * residues :] = mask_ref[0]


def pack_heads(table, mask, gain, weight, heads, scale):
    lines, residues, channels = table.shape
    group = LANES * heads // channels
    packs = lines // group
    rows = 3 * residues + MASK_ROWS
    mask = jnp.pad(mask, ((0, MASK_ROWS - lines), (0, packs * LANES - residues)))
    mask = jnp.transpose(mask.reshape(MASK_ROWS, packs, LANES), (1, 0, 2)).astype(BF16)
    return pl.pallas_call(
        functools.partial(pack_kernel, scale=scale),
        grid=(packs,),
        in_specs=[
            pl.BlockSpec((group, residues, channels), lambda s: (s, 0, 0)),
            pl.BlockSpec((1, MASK_ROWS, LANES), lambda s: (s, 0, 0)),
            pl.BlockSpec((1, channels), lambda s: (0, 0)),
            pl.BlockSpec(weight.shape, lambda s: (0, 0)),
        ],
        out_specs=pl.BlockSpec((heads, 1, rows, LANES), lambda s: (0, s, 0, 0)),
        out_shape=jax.ShapeDtypeStruct((heads, packs, rows, LANES), BF16),
        compiler_params=pltpu.CompilerParams(vmem_limit_bytes=VMEM),
        name="pack_heads",
    )(table, mask, gain[None, :], weight)


TILE = 16


def row_kernel(place_ref, own_ref, other_ref, *rest, turn, count, residues, head_size):
    bias_refs, rest = rest[:count], rest[count:]
    out_ref, bias32_ref, key_ref, value_ref, score_ref, weight_ref = rest[-6:]
    earlier = rest[:-6]
    blocks, packs, _, _ = own_ref.shape
    lines, keys, _ = key_ref.shape
    pieces, targets = out_ref.shape[:2]
    span = residues // pieces
    group = LANES // head_size
    chunk = 2 * LANES
    main = 2 * blocks * LANES
    core = place_ref[0]
    there = (place_ref[1] + turn) % 2 * count
    lane8 = lanes_of((EIGHT, LANES))
    lane = lanes_of((residues, LANES))

    for ref in earlier:
        for z in range(ref.shape[1]):
            out_ref[:, place_ref[1] * count + z] = ref[:, z]

    def gather_tails(tails, at):
        total = None
        for e, moved in enumerate(tails):
            if e != at:
                moved = pltpu.roll(moved, ((e - at) * STEP) % LANES, 1)
            total = moved if total is None else jnp.where(lane8 >= e * STEP, moved, total)
        return total

    for block, ref in enumerate(bias_refs):
        for side in range(2):
            parity = core if side == 0 else 1 - core
            for step in range(residues // STEP):
                row = step * STEP
                tails = []
                for k in range(blocks):
                    tile = ref[2 * k + parity, step].astype(F32)
                    column = (side * blocks + k) * LANES
                    bias32_ref[block, row : row + STEP, column : column + LANES] = tile[:STEP]
                    tails.append(tile[STEP:])
                for q in range(blocks // GROUPS):
                    column = main + (side * blocks // GROUPS + q) * LANES
                    for g in range(GROUPS):
                        bias32_ref[block, row + g * EIGHT : row + (g + 1) * EIGHT, column : column + LANES] = (
                            gather_tails(tails[q * GROUPS : (q + 1) * GROUPS], g)
                        )

    def upright(rows):
        wide = jnp.concatenate([rows, jnp.zeros((head_size - lines, LANES), F32)] * group, axis=0)
        return wide.T.astype(BF16)

    lane1 = lanes_of((1, LANES)) // head_size
    for side, ref in enumerate((own_ref, other_ref)):
        for q in range(blocks // GROUPS):
            masks = [ref[q * GROUPS + e, :, 3 * residues :, :].astype(F32) for e in range(GROUPS)]
            rest_mask = upright(gather_tails([m[1, :lines] for m in masks], 0))
            for e in range(GROUPS):
                k = q * GROUPS + e
                first_mask = upright(masks[e][0, :lines])
                head_at = (side * blocks + k) * LANES
                tail_at = main + (side * blocks + k) * STEP
                for pack in range(packs):
                    key = ref[k, pack, residues : 2 * residues, :]
                    value = ref[k, pack, 2 * residues : 3 * residues, :]
                    for member in range(group):
                        s = pack * group + member
                        spare = jnp.where(lane1 == (member + 1) % group, 1.0, 0.0)
                        keep, spare = (1.0 - spare).astype(BF16), spare.astype(BF16)
                        kept = key * keep
                        key_ref[s, head_at : head_at + LANES] = kept[:LANES] + first_mask * spare
                        key_ref[s, tail_at : tail_at + STEP] = (
                            kept[LANES:] + rest_mask[e * STEP : (e + 1) * STEP] * spare
                        )
                        kept = value * keep + spare
                        value_ref[s, head_at : head_at + LANES] = kept[:LANES]
                        value_ref[s, tail_at : tail_at + STEP] = kept[LANES:]

    def body(block, carry):
        ahead = jnp.where(block == 1, -1, jnp.where(block == 2, 1, jnp.where(block == 3, 2, 0)))
        place = there + (place_ref[2] + ahead + count) % count

        def query_of(s):
            member = s % group
            spare = (member + 1) % group * head_size + s
            inside = (lane >= member * head_size) & (lane < (member + 1) * head_size)
            raw = own_ref[place, s // group, :residues, :].astype(F32)
            return jnp.where(inside, raw, jnp.where(lane == spare, 1.0, 0.0)).astype(BF16)

        def score(s, query, j):
            columns = slice(j * chunk, (j + 1) * chunk)
            score_ref[s % 2, :, columns] = dot_nt(query, key_ref[s, columns, :]) + bias32_ref[block, :, columns]

        def weigh(s, row):
            scores = score_ref[s % 2, row : row + TILE, :]
            top = jnp.max(scores, axis=1, keepdims=True)
            weight_ref[s % 2, row : row + TILE, :] = jnp.exp2(scores - top).astype(BF16)

        query = query_of(0)
        for j in range(keys // chunk):
            score(0, query, j)
        total = None
        for s in range(lines):
            member, pack = s % group, s // group
            query = query_of(s + 1) if s + 1 < lines else None
            steps = keys // chunk
            tiles = residues // TILE
            for j in range(steps):
                if query is not None:
                    score(s + 1, query, j)
                for r in range(j * tiles // steps, (j + 1) * tiles // steps):
                    weigh(s, r * TILE)
            mixed = dot(weight_ref[s % 2], value_ref[s])
            spare = (member + 1) % group * head_size
            mixed = mixed / mixed[:, spare : spare + 1]
            total = mixed if member == 0 else jnp.where(lane >= member * head_size, mixed, total)
            if member == group - 1:
                for piece in range(pieces):
                    part = total[piece * span : (piece + 1) * span].astype(BF16)
                    out_ref[piece, place % targets, pack * span : (pack + 1) * span, :] = part
        return carry

    lax.fori_loop(0, count, body, 0)


def row_attention(place, own, other, biases, earlier, turn, residues, pieces, head_size):
    blocks, packs, _, _ = own.shape
    lines = packs * LANES // head_size
    keys = 2 * blocks * residues
    count = len(biases)
    targets = count + sum(e.shape[1] for e in earlier)
    rows = packs * residues // pieces
    scores = lines * count * residues * keys
    return pl.pallas_call(
        functools.partial(row_kernel, turn=turn, count=count, residues=residues, head_size=head_size),
        in_specs=[pl.BlockSpec(memory_space=pltpu.SMEM)]
        + [pl.BlockSpec(memory_space=pltpu.VMEM)] * (2 + count + len(earlier)),
        out_specs=pl.BlockSpec(memory_space=pltpu.VMEM),
        out_shape=jax.ShapeDtypeStruct((pieces, targets, rows, LANES), BF16),
        scratch_shapes=[
            pltpu.VMEM((count, residues, keys), F32),
            pltpu.VMEM((lines, keys, LANES), BF16),
            pltpu.VMEM((lines, keys, LANES), BF16),
            pltpu.VMEM((2, residues, keys), F32),
            pltpu.VMEM((2, residues, keys), BF16),
        ],
        compiler_params=pltpu.CompilerParams(vmem_limit_bytes=ROW_VMEM),
        cost_estimate=pl.CostEstimate(flops=scores * 512, bytes_accessed=12_000_000, transcendentals=scores),
        name="row_attention",
    )(place, own, other, *biases, *earlier)


def column_kernel(
    mixed_ref, table_ref, mask_ref,
    row_gain_ref, row_gate_ref, row_shift_ref, row_out_ref, row_bias_ref,
    col_gain_ref, col_weight_ref, col_shift_ref, col_out_ref, col_bias_ref,
    ff_gain_ref, expand_ref, shrink_ref, out_ref, mixed32_ref, *, heads, scale,
):
    groups, span, lines, channels = table_ref.shape
    rows = groups * lines
    head_size = channels // heads

    @pl.when(pl.program_id(0) == 0)
    def _():
        members = LANES // head_size
        packs = lines // members
        received = mixed_ref.shape[2]
        residues = received // packs
        source = lax.broadcasted_iota(jnp.int32, (LANES, channels), 0)
        target = lanes_of((LANES, channels))
        tokens = [mixed_ref[:, h].astype(F32).reshape(groups * received, LANES).astype(BF16) for h in range(heads)]
        for member in range(members):
            total = None
            for h in range(heads):
                move = (target // head_size == h) & (source == target - h * head_size + member * head_size)
                part = dot(tokens[h], jnp.where(move, 1.0, 0.0).astype(BF16))
                total = part if total is None else total + part
            for r in range(groups):
                for pack in range(packs):
                    row = r * received + pack * residues
                    line = r * lines + pack * members + member
                    for part in range(channels // LANES):
                        mixed32_ref[part, pl.ds(line, residues, stride=rows), :] = total[
                            row : row + residues, part * LANES : (part + 1) * LANES
                        ]

    table = table_ref[...].astype(F32)
    table = jnp.concatenate([table[:, i].reshape(rows, channels) for i in range(span)], axis=0)
    here = pl.ds(pl.program_id(0) * span * rows, span * rows)
    mixed = jnp.concatenate([mixed32_ref[part, here, :] for part in range(channels // LANES)], axis=1)

    row_in = normalize(table, row_gain_ref[...]).astype(BF16)
    gate = jax.nn.sigmoid(dot(row_in, row_gate_ref[...]) + row_shift_ref[...])
    gated = (mixed * gate).astype(BF16)
    after_rows = table + (dot(gated, row_out_ref[...]) + row_bias_ref[...])
    after_rows = after_rows.astype(BF16).astype(F32)

    col_in = normalize(after_rows, col_gain_ref[...]).astype(BF16)
    projected = dot(col_in, col_weight_ref[...])
    query = (projected[:, :channels] * scale).astype(BF16)
    key = projected[:, channels : 2 * channels].astype(BF16)
    value = projected[:, 2 * channels : 3 * channels].astype(BF16)
    gate = jax.nn.sigmoid(projected[:, 3 * channels :] + col_shift_ref[...])

    shape = (heads * rows, channels)
    row_head = lax.broadcasted_iota(jnp.int32, shape, 0) // rows
    same = row_head == lax.broadcasted_iota(jnp.int32, shape, 1) // head_size
    same = jnp.where(same, 1.0, 0.0).astype(BF16)
    masks = mask_ref[:, 0].astype(F32).reshape(rows, channels)
    mask_lane = lanes_of((rows, channels))
    attended = []
    for i in range(span):
        here = slice(i * rows, (i + 1) * rows)
        spread_key = jnp.concatenate([key[here]] * heads, axis=0) * same
        spread_value = jnp.concatenate([value[here]] * heads, axis=0) * same
        scores = dot_nt(spread_key, query[here]).reshape(heads, rows, rows)
        place = pl.program_id(0) * span + i
        present = jnp.sum(jnp.where(mask_lane == place, masks, 0.0), axis=1, keepdims=True)
        scores = jnp.where(present[None] > 0, scores, -1e9)
        top = jnp.max(scores, axis=1, keepdims=True)
        weights = jnp.exp2(scores - top)
        weights = weights / jnp.sum(weights, axis=1, keepdims=True)
        weights = weights.astype(BF16).reshape(heads * rows, rows)
        attended.append(dot_tn(weights, spread_value))
    gated = (jnp.concatenate(attended, axis=0) * gate).astype(BF16)
    after_cols = after_rows + (dot(gated, col_out_ref[...]) + col_bias_ref[...])
    after_cols = after_cols.astype(BF16).astype(F32)

    trans_in = normalize(after_cols, ff_gain_ref[...]).astype(BF16)
    hidden = jnp.maximum(dot(trans_in, expand_ref[...]), 0.0).astype(BF16)
    updated = after_cols + dot(hidden, shrink_ref[...])
    for i in range(span):
        block = updated[i * rows : (i + 1) * rows].reshape(groups, lines, channels)
        out_ref[:, i] = block.astype(BF16)


def column_phase(mixed, table, params, heads, scale, span):
    groups, extended, lines, channels = table.shape
    residues = extended - 1
    token_block = pl.BlockSpec((groups, span, lines, channels), lambda i: (0, i, 0, 0))
    in_specs = [
        pl.BlockSpec(mixed.shape, lambda i: (0, 0, 0, 0)),
        token_block,
        pl.BlockSpec((groups, 1, lines, channels), lambda i: (0, residues, 0, 0)),
    ]
    in_specs += [pl.BlockSpec(p.shape, lambda i: (0, 0)) for p in params]
    return pl.pallas_call(
        functools.partial(column_kernel, heads=heads, scale=scale),
        grid=(residues // span,),
        in_specs=in_specs,
        out_specs=token_block,
        out_shape=jax.ShapeDtypeStruct((groups, residues, lines, channels), BF16),
        scratch_shapes=[pltpu.VMEM((channels // LANES, residues * groups * lines, LANES), F32)],
        compiler_params=pltpu.CompilerParams(vmem_limit_bytes=VMEM),
        name="column_phase",
    )(mixed, table, table, *params)


def shards(
    seq_size,
    res_size,
    homology_table,
    coupled_state,
    aligned_indicator,
    amino_indicator,
    horizontal_scaling_factor,
    horizontal_projection_matrix,
    horizontal_sigmoid_shift,
    horizontal_result_matrix,
    horizontal_result_shift,
    coupling_scaling_factor,
    coupling_head_matrix,
    downward_stretch_vector,
    vertical_projection_matrix,
    vertical_sigmoid_shift,
    vertical_result_matrix,
    vertical_result_shift,
    feedforward_scaling_factor,
    feedforward_expand_matrix,
    feedforward_shrink_matrix,
):
    lines, residues, channels = homology_table.shape
    heads = coupling_head_matrix.shape[1]
    head_size = channels // heads
    scale = LOG2E / math.sqrt(head_size)
    span = residues // seq_size
    core = lax.axis_index("res") % 2
    parity = [list(range(p, res_size, 2)) for p in (0, 1)]
    parity_all = [[r * res_size + c for r in range(seq_size) for c in group] for group in parity]

    tile_bias = pair_bias(coupled_state, coupling_scaling_factor, coupling_head_matrix)
    tile_bias, homology_table = lax.optimization_barrier((tile_bias, homology_table))
    steps = tile_bias.shape[1] // 2
    near = lax.all_to_all(tile_bias.reshape(res_size, steps, STEP_ROWS, LANES), "res", 0, 0)

    by_residue = jnp.transpose(homology_table, (1, 0, 2)).reshape(seq_size, span, lines, channels)
    mask_row = jnp.transpose(aligned_indicator.reshape(lines, seq_size, span), (1, 0, 2))
    mask_row = jnp.pad(mask_row.astype(BF16), ((0, 0), (0, 0), (0, channels - span)))
    columns = jnp.concatenate([by_residue, mask_row[:, None]], axis=1)

    present = aligned_indicator * amino_indicator[None, :]
    mask = jnp.where(present > 0, 0.0, MASKED).astype(F32)
    packed = pack_heads(
        homology_table, mask, horizontal_scaling_factor, horizontal_projection_matrix, heads, scale
    )
    me = lax.axis_index("seq")
    place = jnp.stack([core, me // (seq_size // 2), me % (seq_size // 2)]).astype(jnp.int32)
    near, packed, columns, place = lax.optimization_barrier((near, packed, columns, place))
    own = lax.all_to_all(packed, "res", 0, 0, axis_index_groups=parity)

    ring = seq_size // 2

    def around(values, by):
        return lax.ppermute(
            values, "seq", [(h * ring + z, h * ring + (z + by) % ring) for h in (0, 1) for z in range(ring)]
        )

    def swap(values):
        return lax.ppermute(values, "seq", [(r, (r + ring) % seq_size) for r in range(seq_size)])

    up, down, far = around(near, 1), around(near, -1), swap(near)
    across = around(up, 1)
    own, up, down, far, across = lax.optimization_barrier((own, up, down, far, across))
    other = lax.ppermute(own, "res", [(c, c ^ 1) for c in range(res_size)])
    near_biases = [near, up, down, across]
    far_biases = [far, around(far, 1), around(far, -1), swap(across)]

    mixed = row_attention(place, own, other, near_biases, [], 0, residues, seq_size, head_size)
    columns = lax.all_to_all(columns, "seq", 0, 0)
    mixed, columns = lax.optimization_barrier((mixed, columns))
    mixed = row_attention(place, own, other, far_biases, [mixed], 1, residues, seq_size, head_size)
    mixed = mixed.reshape((seq_size * ring * 2,) + mixed.shape[2:])
    mixed = lax.all_to_all(mixed, ("seq", "res"), 0, 0, axis_index_groups=parity_all)
    mixed = mixed.reshape((seq_size, heads) + mixed.shape[1:])

    params = [
        horizontal_scaling_factor[None],
        horizontal_projection_matrix[:, 3 * channels :],
        horizontal_sigmoid_shift[None],
        horizontal_result_matrix,
        horizontal_result_shift[None],
        downward_stretch_vector[None],
        vertical_projection_matrix,
        vertical_sigmoid_shift[None],
        vertical_result_matrix,
        vertical_result_shift[None],
        feedforward_scaling_factor[None],
        feedforward_expand_matrix,
        feedforward_shrink_matrix,
    ]
    updated = column_phase(mixed, columns, params, heads, scale, span)
    updated = lax.all_to_all(updated, "seq", 0, 0)
    return jnp.transpose(updated.reshape(residues, lines, channels), (1, 0, 2))


def solution(mesh):
    table = P("seq", "res", None)
    return jax.shard_map(
        functools.partial(shards, mesh.shape["seq"], mesh.shape["res"]),
        mesh=mesh,
        in_specs=(table, table, P("seq", "res"), P("res")) + (P(),) * 15,
        out_specs=table,
        check_vma=False,
    )
```

```python
import functools
import math

import jax
import jax.numpy as jnp
from jax import lax
from jax.experimental import pallas as pl
from jax.experimental.pallas import tpu as pltpu
from jax.sharding import PartitionSpec as P

F32 = jnp.float32
BF16 = jnp.bfloat16
EPS = 1e-05
LOG2E = 1.4426950408889634
LANES = 128
MASKED = -1e30
VMEM = 56 * 2**20
LESS_VMEM = 40 * 2**20


def dot(a, b):
    return jnp.dot(a, b, preferred_element_type=F32)


def dot_nt(a, b):
    return lax.dot_general(a, b, (((1,), (1,)), ((), ())), preferred_element_type=F32)


def dot_tn(a, b):
    return lax.dot_general(a, b, (((0,), (0,)), ((), ())), preferred_element_type=F32)


def normalize(values, gain):
    center = values - jnp.mean(values, axis=-1, keepdims=True)
    spread = jnp.mean(center * center, axis=-1, keepdims=True)
    return center * lax.rsqrt(spread + EPS) * gain


def lanes_of(shape):
    return lax.broadcasted_iota(jnp.int32, shape, len(shape) - 1)


STEP = 32
GROUPS = 4
EIGHT = 8
STEP_ROWS = STEP + EIGHT


def pair_kernel(pair_ref, gain_ref, head_ref, bias_ref, project_ref, rows_ref):
    channels, heads = head_ref.shape

    @pl.when(pl.program_id(0) == 0)
    def _():
        gained = (gain_ref[...] * LOG2E) * head_ref[...].astype(F32).T
        gained = gained - jnp.mean(gained, axis=1, keepdims=True)
        high = gained.astype(BF16)
        low = (gained - high.astype(F32)).astype(BF16)
        same = lax.broadcasted_iota(jnp.int32, (channels, channels), 0) == lanes_of((channels, channels))
        centering = jnp.where(same, 1.0, 0.0) - 1.0 / channels
        project_ref[:channels] = centering.astype(BF16)
        project_ref[channels:] = jnp.concatenate([high.astype(F32), low.astype(F32)], axis=0).astype(BF16)

    def project(tokens):
        both = dot_nt(project_ref[...], tokens)
        center = both[:channels]
        spread = jnp.sum(center * center, axis=0, keepdims=True) * (1.0 / channels)
        raw = both[channels : channels + heads] + both[channels + heads :]
        return raw * lax.rsqrt(spread + EPS)

    for part in range(bias_ref.shape[1]):
        row, at = part * STEP, part * STEP_ROWS
        for i in range(0, STEP, 2):
            done = project(pair_ref[row + i : row + i + 2, :LANES, :].reshape(2 * LANES, channels))
            rows_ref[:, at + i, :] = done[:, :LANES]
            rows_ref[:, at + i + 1, :] = done[:, LANES:]
        for r in range(0, EIGHT, 2):
            rest = [pair_ref[row + g * EIGHT + r + e, LANES:, :] for e in range(2) for g in range(GROUPS)]
            done = project(jnp.concatenate(rest, axis=0))
            rows_ref[:, at + STEP + r, :] = done[:, :LANES]
            rows_ref[:, at + STEP + r + 1, :] = done[:, LANES:]
    for part in range(bias_ref.shape[1]):
        bias_ref[:, part] = rows_ref[:, part * STEP_ROWS : (part + 1) * STEP_ROWS].astype(BF16)


def pair_bias(coupled, gain, head_matrix, parts):
    rows, cols, channels = coupled.shape
    heads = head_matrix.shape[1]
    return pl.pallas_call(
        pair_kernel,
        grid=(rows // STEP // parts,),
        in_specs=[
            pl.BlockSpec((parts * STEP, cols, channels), lambda i: (i, 0, 0)),
            pl.BlockSpec((1, channels), lambda i: (0, 0)),
            pl.BlockSpec((channels, heads), lambda i: (0, 0)),
        ],
        out_specs=pl.BlockSpec((heads, parts, STEP_ROWS, LANES), lambda i: (0, i, 0, 0)),
        out_shape=jax.ShapeDtypeStruct((heads, rows // STEP, STEP_ROWS, LANES), BF16),
        scratch_shapes=[
            pltpu.VMEM((channels + 2 * heads, channels), BF16),
            pltpu.VMEM((heads, parts * STEP_ROWS, LANES), F32),
        ],
        compiler_params=pltpu.CompilerParams(vmem_limit_bytes=VMEM),
        name="pair_bias",
    )(coupled, gain[None], head_matrix)


MASK_ROWS = 16


def pack_kernel(table_ref, mask_ref, gain_ref, weight_ref, packed_ref, *, scale):
    group, residues, channels = table_ref.shape
    heads = packed_ref.shape[0]
    head_size = channels // heads
    lane = lanes_of((residues, LANES))
    flat = []
    for member in range(group):
        normed = normalize(table_ref[member].astype(F32), gain_ref[...]).astype(BF16)
        flat.append(dot(normed, weight_ref[:, : 3 * channels]))
    for h in range(heads):
        for kind in range(3):
            column = kind * channels + h // group * LANES
            total = None
            for member in range(group):
                part = flat[member][:, column : column + LANES]
                if member != h % group:
                    part = pltpu.roll(part, ((member - h % group) * head_size) % LANES, 1)
                total = part if total is None else jnp.where(lane >= member * head_size, part, total)
            if kind == 0:
                total = total * scale
            packed_ref[h, 0, kind * residues : (kind + 1) * residues] = total.astype(BF16)
        packed_ref[h, 0, 3 * residues :] = mask_ref[0]


def pack_heads(table, mask, gain, weight, heads, scale):
    lines, residues, channels = table.shape
    group = LANES * heads // channels
    packs = lines // group
    rows = 3 * residues + MASK_ROWS
    mask = jnp.pad(mask, ((0, MASK_ROWS - lines), (0, packs * LANES - residues)))
    mask = jnp.transpose(mask.reshape(MASK_ROWS, packs, LANES), (1, 0, 2)).astype(BF16)
    return pl.pallas_call(
        functools.partial(pack_kernel, scale=scale),
        grid=(packs,),
        in_specs=[
            pl.BlockSpec((group, residues, channels), lambda s: (s, 0, 0)),
            pl.BlockSpec((1, MASK_ROWS, LANES), lambda s: (s, 0, 0)),
            pl.BlockSpec((1, channels), lambda s: (0, 0)),
            pl.BlockSpec(weight.shape, lambda s: (0, 0)),
        ],
        out_specs=pl.BlockSpec((heads, 1, rows, LANES), lambda s: (0, s, 0, 0)),
        out_shape=jax.ShapeDtypeStruct((heads, packs, rows, LANES), BF16),
        compiler_params=pltpu.CompilerParams(vmem_limit_bytes=VMEM),
        name="pack_heads",
    )(table, mask, gain[None, :], weight)


TILE = 16


def row_kernel(place_ref, own_ref, other_ref, *rest, turn, count, residues, head_size):
    bias_refs, rest = rest[:count], rest[count:]
    out_ref, bias32_ref, key_ref, value_ref, score_ref, weight_ref = rest[-6:]
    earlier = rest[:-6]
    blocks, packs, _, _ = own_ref.shape
    lines, keys, _ = key_ref.shape
    pieces, targets = out_ref.shape[:2]
    span = residues // pieces
    group = LANES // head_size
    chunk = 2 * LANES
    main = 2 * blocks * LANES
    core = place_ref[0]
    there = (place_ref[1] + turn) % 2 * count
    lane8 = lanes_of((EIGHT, LANES))
    lane = lanes_of((residues, LANES))

    for ref in earlier:
        for z in range(ref.shape[1]):
            out_ref[:, place_ref[1] * count + z] = ref[:, z]

    def gather_tails(tails, at):
        total = None
        for e, moved in enumerate(tails):
            if e != at:
                moved = pltpu.roll(moved, ((e - at) * STEP) % LANES, 1)
            total = moved if total is None else jnp.where(lane8 >= e * STEP, moved, total)
        return total

    for block, ref in enumerate(bias_refs):
        for side in range(2):
            parity = core if side == 0 else 1 - core
            for step in range(residues // STEP):
                row = step * STEP
                tails = []
                for k in range(blocks):
                    tile = ref[2 * k + parity, step].astype(F32)
                    column = (side * blocks + k) * LANES
                    bias32_ref[block, row : row + STEP, column : column + LANES] = tile[:STEP]
                    tails.append(tile[STEP:])
                for q in range(blocks // GROUPS):
                    column = main + (side * blocks // GROUPS + q) * LANES
                    for g in range(GROUPS):
                        bias32_ref[block, row + g * EIGHT : row + (g + 1) * EIGHT, column : column + LANES] = (
                            gather_tails(tails[q * GROUPS : (q + 1) * GROUPS], g)
                        )

    def upright(rows):
        wide = jnp.concatenate([rows, jnp.zeros((head_size - lines, LANES), F32)] * group, axis=0)
        return wide.T.astype(BF16)

    lane1 = lanes_of((1, LANES)) // head_size
    for side, ref in enumerate((own_ref, other_ref)):
        for q in range(blocks // GROUPS):
            masks = [ref[q * GROUPS + e, :, 3 * residues :, :].astype(F32) for e in range(GROUPS)]
            rest_mask = upright(gather_tails([m[1, :lines] for m in masks], 0))
            for e in range(GROUPS):
                k = q * GROUPS + e
                first_mask = upright(masks[e][0, :lines])
                head_at = (side * blocks + k) * LANES
                tail_at = main + (side * blocks + k) * STEP
                for pack in range(packs):
                    key = ref[k, pack, residues : 2 * residues, :]
                    value = ref[k, pack, 2 * residues : 3 * residues, :]
                    for member in range(group):
                        s = pack * group + member
                        spare = jnp.where(lane1 == (member + 1) % group, 1.0, 0.0)
                        keep, spare = (1.0 - spare).astype(BF16), spare.astype(BF16)
                        kept = key * keep
                        key_ref[s, head_at : head_at + LANES] = kept[:LANES] + first_mask * spare
                        key_ref[s, tail_at : tail_at + STEP] = (
                            kept[LANES:] + rest_mask[e * STEP : (e + 1) * STEP] * spare
                        )
                        kept = value * keep + spare
                        value_ref[s, head_at : head_at + LANES] = kept[:LANES]
                        value_ref[s, tail_at : tail_at + STEP] = kept[LANES:]

    def body(block, carry):
        ahead = jnp.where(block == 1, -1, jnp.where(block == 2, 1, jnp.where(block == 3, 2, 0)))
        place = there + (place_ref[2] + ahead + count) % count

        def query_of(s):
            member = s % group
            spare = (member + 1) % group * head_size + s
            inside = (lane >= member * head_size) & (lane < (member + 1) * head_size)
            raw = own_ref[place, s // group, :residues, :].astype(F32)
            return jnp.where(inside, raw, jnp.where(lane == spare, 1.0, 0.0)).astype(BF16)

        def score(s, query, j):
            columns = slice(j * chunk, (j + 1) * chunk)
            score_ref[s % 2, :, columns] = dot_nt(query, key_ref[s, columns, :]) + bias32_ref[block, :, columns]

        def weigh(s, row):
            scores = score_ref[s % 2, row : row + TILE, :]
            top = jnp.max(scores, axis=1, keepdims=True)
            weight_ref[s % 2, row : row + TILE, :] = jnp.exp2(scores - top).astype(BF16)

        query = query_of(0)
        for j in range(keys // chunk):
            score(0, query, j)
        total = None
        for s in range(lines):
            member, pack = s % group, s // group
            query = query_of(s + 1) if s + 1 < lines else None
            steps = keys // chunk
            tiles = residues // TILE
            for j in range(steps):
                if query is not None:
                    score(s + 1, query, j)
                for r in range(j * tiles // steps, (j + 1) * tiles // steps):
                    weigh(s, r * TILE)
            mixed = dot(weight_ref[s % 2], value_ref[s])
            spare = (member + 1) % group * head_size
            mixed = mixed / mixed[:, spare : spare + 1]
            total = mixed if member == 0 else jnp.where(lane >= member * head_size, mixed, total)
            if member == group - 1:
                for piece in range(pieces):
                    part = total[piece * span : (piece + 1) * span].astype(BF16)
                    out_ref[piece, place % targets, pack * span : (pack + 1) * span, :] = part
        return carry

    lax.fori_loop(0, count, body, 0)


def row_attention(place, own, other, biases, earlier, turn, residues, pieces, head_size):
    blocks, packs, _, _ = own.shape
    lines = packs * LANES // head_size
    keys = 2 * blocks * residues
    count = len(biases)
    targets = count + sum(e.shape[1] for e in earlier)
    rows = packs * residues // pieces
    scores = lines * count * residues * keys
    return pl.pallas_call(
        functools.partial(row_kernel, turn=turn, count=count, residues=residues, head_size=head_size),
        in_specs=[pl.BlockSpec(memory_space=pltpu.SMEM)]
        + [pl.BlockSpec(memory_space=pltpu.VMEM)] * (2 + count + len(earlier)),
        out_specs=pl.BlockSpec(memory_space=pltpu.VMEM),
        out_shape=jax.ShapeDtypeStruct((pieces, targets, rows, LANES), BF16),
        scratch_shapes=[
            pltpu.VMEM((count, residues, keys), F32),
            pltpu.VMEM((lines, keys, LANES), BF16),
            pltpu.VMEM((lines, keys, LANES), BF16),
            pltpu.VMEM((2, residues, keys), F32),
            pltpu.VMEM((2, residues, keys), BF16),
        ],
        compiler_params=pltpu.CompilerParams(vmem_limit_bytes=LESS_VMEM),
        cost_estimate=pl.CostEstimate(flops=scores * 512, bytes_accessed=12_000_000, transcendentals=scores),
        name="row_attention",
    )(place, own, other, *biases, *earlier)


def column_kernel(
    mixed_ref, table_ref, mask_ref,
    row_gain_ref, row_gate_ref, row_shift_ref, row_out_ref, row_bias_ref,
    col_gain_ref, col_weight_ref, col_shift_ref, col_out_ref, col_bias_ref,
    ff_gain_ref, expand_ref, shrink_ref, out_ref, mixed32_ref, *, heads, scale,
):
    groups, span, lines, channels = table_ref.shape
    rows = groups * lines
    head_size = channels // heads

    @pl.when(pl.program_id(0) == 0)
    def _():
        members = LANES // head_size
        packs = lines // members
        received = mixed_ref.shape[2]
        residues = received // packs
        source = lax.broadcasted_iota(jnp.int32, (LANES, channels), 0)
        target = lanes_of((LANES, channels))
        tokens = [mixed_ref[:, h].astype(F32).reshape(groups * received, LANES).astype(BF16) for h in range(heads)]
        for member in range(members):
            total = None
            for h in range(heads):
                move = (target // head_size == h) & (source == target - h * head_size + member * head_size)
                part = dot(tokens[h], jnp.where(move, 1.0, 0.0).astype(BF16))
                total = part if total is None else total + part
            for r in range(groups):
                for pack in range(packs):
                    row = r * received + pack * residues
                    line = r * lines + pack * members + member
                    for part in range(channels // LANES):
                        mixed32_ref[part, pl.ds(line, residues, stride=rows), :] = total[
                            row : row + residues, part * LANES : (part + 1) * LANES
                        ]

    table = table_ref[...].astype(F32)
    table = jnp.concatenate([table[:, i].reshape(rows, channels) for i in range(span)], axis=0)
    here = pl.ds(pl.program_id(0) * span * rows, span * rows)
    mixed = jnp.concatenate([mixed32_ref[part, here, :] for part in range(channels // LANES)], axis=1)

    row_in = normalize(table, row_gain_ref[...]).astype(BF16)
    gate = jax.nn.sigmoid(dot(row_in, row_gate_ref[...]) + row_shift_ref[...])
    gated = (mixed * gate).astype(BF16)
    after_rows = table + (dot(gated, row_out_ref[...]) + row_bias_ref[...])
    after_rows = after_rows.astype(BF16).astype(F32)

    col_in = normalize(after_rows, col_gain_ref[...]).astype(BF16)
    projected = dot(col_in, col_weight_ref[...])
    query = (projected[:, :channels] * scale).astype(BF16)
    key = projected[:, channels : 2 * channels].astype(BF16)
    value = projected[:, 2 * channels : 3 * channels].astype(BF16)
    gate = jax.nn.sigmoid(projected[:, 3 * channels :] + col_shift_ref[...])

    shape = (heads * rows, channels)
    row_head = lax.broadcasted_iota(jnp.int32, shape, 0) // rows
    same = row_head == lax.broadcasted_iota(jnp.int32, shape, 1) // head_size
    same = jnp.where(same, 1.0, 0.0).astype(BF16)
    masks = mask_ref[:, 0].astype(F32).reshape(rows, channels)
    mask_lane = lanes_of((rows, channels))
    attended = []
    for i in range(span):
        here = slice(i * rows, (i + 1) * rows)
        spread_key = jnp.concatenate([key[here]] * heads, axis=0) * same
        spread_value = jnp.concatenate([value[here]] * heads, axis=0) * same
        scores = dot_nt(spread_key, query[here]).reshape(heads, rows, rows)
        place = pl.program_id(0) * span + i
        present = jnp.sum(jnp.where(mask_lane == place, masks, 0.0), axis=1, keepdims=True)
        scores = jnp.where(present[None] > 0, scores, -1e9)
        top = jnp.max(scores, axis=1, keepdims=True)
        weights = jnp.exp2(scores - top)
        weights = weights / jnp.sum(weights, axis=1, keepdims=True)
        weights = weights.astype(BF16).reshape(heads * rows, rows)
        attended.append(dot_tn(weights, spread_value))
    gated = (jnp.concatenate(attended, axis=0) * gate).astype(BF16)
    after_cols = after_rows + (dot(gated, col_out_ref[...]) + col_bias_ref[...])
    after_cols = after_cols.astype(BF16).astype(F32)

    trans_in = normalize(after_cols, ff_gain_ref[...]).astype(BF16)
    hidden = jnp.maximum(dot(trans_in, expand_ref[...]), 0.0).astype(BF16)
    updated = after_cols + dot(hidden, shrink_ref[...])
    for i in range(span):
        block = updated[i * rows : (i + 1) * rows].reshape(groups, lines, channels)
        out_ref[:, i] = block.astype(BF16)


def column_phase(mixed, table, params, heads, scale, span):
    groups, extended, lines, channels = table.shape
    residues = extended - 1
    token_block = pl.BlockSpec((groups, span, lines, channels), lambda i: (0, i, 0, 0))
    in_specs = [
        pl.BlockSpec(mixed.shape, lambda i: (0, 0, 0, 0)),
        token_block,
        pl.BlockSpec((groups, 1, lines, channels), lambda i: (0, residues, 0, 0)),
    ]
    in_specs += [pl.BlockSpec(p.shape, lambda i: (0, 0)) for p in params]
    return pl.pallas_call(
        functools.partial(column_kernel, heads=heads, scale=scale),
        grid=(residues // span,),
        in_specs=in_specs,
        out_specs=token_block,
        out_shape=jax.ShapeDtypeStruct((groups, residues, lines, channels), BF16),
        scratch_shapes=[pltpu.VMEM((channels // LANES, residues * groups * lines, LANES), F32)],
        compiler_params=pltpu.CompilerParams(vmem_limit_bytes=LESS_VMEM),
        name="column_phase",
    )(mixed, table, table, *params)


def shards(
    seq_size,
    res_size,
    homology_table,
    coupled_state,
    aligned_indicator,
    amino_indicator,
    horizontal_scaling_factor,
    horizontal_projection_matrix,
    horizontal_sigmoid_shift,
    horizontal_result_matrix,
    horizontal_result_shift,
    coupling_scaling_factor,
    coupling_head_matrix,
    downward_stretch_vector,
    vertical_projection_matrix,
    vertical_sigmoid_shift,
    vertical_result_matrix,
    vertical_result_shift,
    feedforward_scaling_factor,
    feedforward_expand_matrix,
    feedforward_shrink_matrix,
):
    lines, residues, channels = homology_table.shape
    heads = coupling_head_matrix.shape[1]
    head_size = channels // heads
    scale = LOG2E / math.sqrt(head_size)
    span = residues // seq_size
    core = lax.axis_index("res") % 2
    parity = [list(range(p, res_size, 2)) for p in (0, 1)]
    parity_all = [[r * res_size + c for r in range(seq_size) for c in group] for group in parity]

    tile_bias = pair_bias(coupled_state, coupling_scaling_factor, coupling_head_matrix, residues // STEP)
    tile_bias, homology_table = lax.optimization_barrier((tile_bias, homology_table))
    steps = tile_bias.shape[1] // 2
    near = lax.all_to_all(tile_bias.reshape(res_size, steps, STEP_ROWS, LANES), "res", 0, 0)

    by_residue = jnp.transpose(homology_table, (1, 0, 2)).reshape(seq_size, span, lines, channels)
    mask_row = jnp.transpose(aligned_indicator.reshape(lines, seq_size, span), (1, 0, 2))
    mask_row = jnp.pad(mask_row.astype(BF16), ((0, 0), (0, 0), (0, channels - span)))
    columns = jnp.concatenate([by_residue, mask_row[:, None]], axis=1)

    present = aligned_indicator * amino_indicator[None, :]
    mask = jnp.where(present > 0, 0.0, MASKED).astype(F32)
    packed = pack_heads(
        homology_table, mask, horizontal_scaling_factor, horizontal_projection_matrix, heads, scale
    )
    me = lax.axis_index("seq")
    place = jnp.stack([core, me // (seq_size // 2), me % (seq_size // 2)]).astype(jnp.int32)
    near, packed, columns, place = lax.optimization_barrier((near, packed, columns, place))
    own = lax.all_to_all(packed, "res", 0, 0, axis_index_groups=parity)

    ring = seq_size // 2

    def around(values, by):
        return lax.ppermute(
            values, "seq", [(h * ring + z, h * ring + (z + by) % ring) for h in (0, 1) for z in range(ring)]
        )

    def swap(values):
        return lax.ppermute(values, "seq", [(r, (r + ring) % seq_size) for r in range(seq_size)])

    up, down, far = around(near, 1), around(near, -1), swap(near)
    across = around(up, 1)
    own, up, down, far, across = lax.optimization_barrier((own, up, down, far, across))
    other = lax.ppermute(own, "res", [(c, c ^ 1) for c in range(res_size)])
    near_biases = [near, up, down, across]
    far_biases = [far, around(far, 1), around(far, -1), swap(across)]

    mixed = row_attention(place, own, other, near_biases, [], 0, residues, seq_size, head_size)
    columns = lax.all_to_all(columns, "seq", 0, 0)
    mixed, columns = lax.optimization_barrier((mixed, columns))
    mixed = row_attention(place, own, other, far_biases, [mixed], 1, residues, seq_size, head_size)
    mixed = mixed.reshape((seq_size * ring * 2,) + mixed.shape[2:])
    mixed = lax.all_to_all(mixed, ("seq", "res"), 0, 0, axis_index_groups=parity_all)
    mixed = mixed.reshape((seq_size, heads) + mixed.shape[1:])

    params = [
        horizontal_scaling_factor[None],
        horizontal_projection_matrix[:, 3 * channels :],
        horizontal_sigmoid_shift[None],
        horizontal_result_matrix,
        horizontal_result_shift[None],
        downward_stretch_vector[None],
        vertical_projection_matrix,
        vertical_sigmoid_shift[None],
        vertical_result_matrix,
        vertical_result_shift[None],
        feedforward_scaling_factor[None],
        feedforward_expand_matrix,
        feedforward_shrink_matrix,
    ]
    updated = column_phase(mixed, columns, params, heads, scale, span)
    updated = lax.all_to_all(updated, "seq", 0, 0)
    return jnp.transpose(updated.reshape(residues, lines, channels), (1, 0, 2))


def solution(mesh):
    table = P("seq", "res", None)
    return jax.shard_map(
        functools.partial(shards, mesh.shape["seq"], mesh.shape["res"]),
        mesh=mesh,
        in_specs=(table, table, P("seq", "res"), P("res")) + (P(),) * 15,
        out_specs=table,
        check_vma=False,
    )
```

```python
import functools
import math

import jax
import jax.numpy as jnp
from jax import lax
from jax.experimental import pallas as pl
from jax.experimental.pallas import tpu as pltpu
from jax.sharding import PartitionSpec as P

F32 = jnp.float32
BF16 = jnp.bfloat16
EPS = 1e-05
LOG2E = 1.4426950408889634
LANES = 128
MASKED = -1e30
VMEM = 56 * 2**20
LESS_VMEM = 40 * 2**20


def dot(a, b):
    return jnp.dot(a, b, preferred_element_type=F32)


def dot_nt(a, b):
    return lax.dot_general(a, b, (((1,), (1,)), ((), ())), preferred_element_type=F32)


def dot_tn(a, b):
    return lax.dot_general(a, b, (((0,), (0,)), ((), ())), preferred_element_type=F32)


def normalize(values, gain):
    center = values - jnp.mean(values, axis=-1, keepdims=True)
    spread = jnp.mean(center * center, axis=-1, keepdims=True)
    return center * lax.rsqrt(spread + EPS) * gain


def lanes_of(shape):
    return lax.broadcasted_iota(jnp.int32, shape, len(shape) - 1)


STEP = 32
GROUPS = 4
EIGHT = 8
STEP_ROWS = STEP + EIGHT


def pair_kernel(pair_ref, gain_ref, head_ref, bias_ref, project_ref, rows_ref):
    heads, channels = head_ref.shape

    @pl.when(pl.program_id(0) == 0)
    def _():
        gained = (gain_ref[...] * LOG2E) * head_ref[...].astype(F32)
        gained = gained - jnp.mean(gained, axis=1, keepdims=True)
        high = gained.astype(BF16)
        low = (gained - high.astype(F32)).astype(BF16)
        same = lax.broadcasted_iota(jnp.int32, (channels, channels), 0) == lanes_of((channels, channels))
        centering = jnp.where(same, 1.0, 0.0) - 1.0 / channels
        project_ref[:channels] = centering.astype(BF16)
        project_ref[channels:] = jnp.concatenate([high.astype(F32), low.astype(F32)], axis=0).astype(BF16)

    def project(tokens):
        both = dot_nt(project_ref[...], tokens)
        center = both[:channels]
        spread = jnp.sum(center * center, axis=0, keepdims=True) * (1.0 / channels)
        raw = both[channels : channels + heads] + both[channels + heads :]
        return raw * lax.rsqrt(spread + EPS)

    for part in range(bias_ref.shape[1]):
        row, at = part * STEP, part * STEP_ROWS
        for i in range(0, STEP, 2):
            done = project(pair_ref[row + i : row + i + 2, :LANES, :].reshape(2 * LANES, channels))
            rows_ref[:, at + i, :] = done[:, :LANES]
            rows_ref[:, at + i + 1, :] = done[:, LANES:]
        for r in range(0, EIGHT, 2):
            rest = [pair_ref[row + g * EIGHT + r + e, LANES:, :] for e in range(2) for g in range(GROUPS)]
            done = project(jnp.concatenate(rest, axis=0))
            rows_ref[:, at + STEP + r, :] = done[:, :LANES]
            rows_ref[:, at + STEP + r + 1, :] = done[:, LANES:]
    for part in range(bias_ref.shape[1]):
        bias_ref[:, part] = rows_ref[:, part * STEP_ROWS : (part + 1) * STEP_ROWS].astype(BF16)


def pair_bias(coupled, gain, head_matrix, parts):
    rows, cols, channels = coupled.shape
    heads = head_matrix.shape[1]
    return pl.pallas_call(
        pair_kernel,
        grid=(rows // STEP // parts,),
        in_specs=[
            pl.BlockSpec((parts * STEP, cols, channels), lambda i: (i, 0, 0)),
            pl.BlockSpec((1, channels), lambda i: (0, 0)),
            pl.BlockSpec((heads, channels), lambda i: (0, 0)),
        ],
        out_specs=pl.BlockSpec((heads, parts, STEP_ROWS, LANES), lambda i: (0, i, 0, 0)),
        out_shape=jax.ShapeDtypeStruct((heads, rows // STEP, STEP_ROWS, LANES), BF16),
        scratch_shapes=[
            pltpu.VMEM((channels + 2 * heads, channels), BF16),
            pltpu.VMEM((heads, parts * STEP_ROWS, LANES), F32),
        ],
        compiler_params=pltpu.CompilerParams(vmem_limit_bytes=VMEM),
        name="pair_bias",
    )(coupled, gain[None], head_matrix.T)


MASK_ROWS = 16


def pack_kernel(table_ref, mask_ref, gain_ref, weight_ref, packed_ref, *, scale):
    group, residues, channels = table_ref.shape
    heads = packed_ref.shape[0]
    head_size = channels // heads
    lane = lanes_of((residues, LANES))
    flat = []
    for member in range(group):
        normed = normalize(table_ref[member].astype(F32), gain_ref[...]).astype(BF16)
        flat.append(dot(normed, weight_ref[:, : 3 * channels]))
    for h in range(heads):
        for kind in range(3):
            column = kind * channels + h // group * LANES
            total = None
            for member in range(group):
                part = flat[member][:, column : column + LANES]
                if member != h % group:
                    part = pltpu.roll(part, ((member - h % group) * head_size) % LANES, 1)
                total = part if total is None else jnp.where(lane >= member * head_size, part, total)
            if kind == 0:
                total = total * scale
            packed_ref[h, 0, kind * residues : (kind + 1) * residues] = total.astype(BF16)
        packed_ref[h, 0, 3 * residues :] = mask_ref[0]


def pack_heads(table, mask, gain, weight, heads, scale):
    lines, residues, channels = table.shape
    group = LANES * heads // channels
    packs = lines // group
    rows = 3 * residues + MASK_ROWS
    mask = jnp.pad(mask, ((0, MASK_ROWS - lines), (0, packs * LANES - residues)))
    mask = jnp.transpose(mask.reshape(MASK_ROWS, packs, LANES), (1, 0, 2)).astype(BF16)
    return pl.pallas_call(
        functools.partial(pack_kernel, scale=scale),
        grid=(packs,),
        in_specs=[
            pl.BlockSpec((group, residues, channels), lambda s: (s, 0, 0)),
            pl.BlockSpec((1, MASK_ROWS, LANES), lambda s: (s, 0, 0)),
            pl.BlockSpec((1, channels), lambda s: (0, 0)),
            pl.BlockSpec(weight.shape, lambda s: (0, 0)),
        ],
        out_specs=pl.BlockSpec((heads, 1, rows, LANES), lambda s: (0, s, 0, 0)),
        out_shape=jax.ShapeDtypeStruct((heads, packs, rows, LANES), BF16),
        compiler_params=pltpu.CompilerParams(vmem_limit_bytes=VMEM),
        name="pack_heads",
    )(table, mask, gain[None, :], weight)


TILE = 16


def row_kernel(place_ref, own_ref, other_ref, *rest, turn, count, residues, head_size):
    bias_refs, rest = rest[:count], rest[count:]
    out_ref, bias32_ref, key_ref, value_ref, score_ref, weight_ref = rest[-6:]
    earlier = rest[:-6]
    blocks, packs, _, _ = own_ref.shape
    lines, keys, _ = key_ref.shape
    pieces, targets = out_ref.shape[:2]
    span = residues // pieces
    group = LANES // head_size
    chunk = 2 * LANES
    main = 2 * blocks * LANES
    core = place_ref[0]
    there = (place_ref[1] + turn) % 2 * count
    lane8 = lanes_of((EIGHT, LANES))
    lane = lanes_of((residues, LANES))

    for ref in earlier:
        for z in range(ref.shape[1]):
            out_ref[:, place_ref[1] * count + z] = ref[:, z]

    def gather_tails(tails, at):
        total = None
        for e, moved in enumerate(tails):
            if e != at:
                moved = pltpu.roll(moved, ((e - at) * STEP) % LANES, 1)
            total = moved if total is None else jnp.where(lane8 >= e * STEP, moved, total)
        return total

    for block, ref in enumerate(bias_refs):
        for side in range(2):
            parity = core if side == 0 else 1 - core
            for step in range(residues // STEP):
                row = step * STEP
                tails = []
                for k in range(blocks):
                    tile = ref[2 * k + parity, step].astype(F32)
                    column = (side * blocks + k) * LANES
                    bias32_ref[block, row : row + STEP, column : column + LANES] = tile[:STEP]
                    tails.append(tile[STEP:])
                for q in range(blocks // GROUPS):
                    column = main + (side * blocks // GROUPS + q) * LANES
                    for g in range(GROUPS):
                        bias32_ref[block, row + g * EIGHT : row + (g + 1) * EIGHT, column : column + LANES] = (
                            gather_tails(tails[q * GROUPS : (q + 1) * GROUPS], g)
                        )

    def upright(rows):
        wide = jnp.concatenate([rows, jnp.zeros((head_size - lines, LANES), F32)] * group, axis=0)
        return wide.T.astype(BF16)

    lane1 = lanes_of((1, LANES)) // head_size
    for side, ref in enumerate((own_ref, other_ref)):
        for q in range(blocks // GROUPS):
            masks = [ref[q * GROUPS + e, :, 3 * residues :, :].astype(F32) for e in range(GROUPS)]
            rest_mask = upright(gather_tails([m[1, :lines] for m in masks], 0))
            for e in range(GROUPS):
                k = q * GROUPS + e
                first_mask = upright(masks[e][0, :lines])
                head_at = (side * blocks + k) * LANES
                tail_at = main + (side * blocks + k) * STEP
                for pack in range(packs):
                    key = ref[k, pack, residues : 2 * residues, :]
                    value = ref[k, pack, 2 * residues : 3 * residues, :]
                    for member in range(group):
                        s = pack * group + member
                        spare = jnp.where(lane1 == (member + 1) % group, 1.0, 0.0)
                        keep, spare = (1.0 - spare).astype(BF16), spare.astype(BF16)
                        kept = key * keep
                        key_ref[s, head_at : head_at + LANES] = kept[:LANES] + first_mask * spare
                        key_ref[s, tail_at : tail_at + STEP] = (
                            kept[LANES:] + rest_mask[e * STEP : (e + 1) * STEP] * spare
                        )
                        kept = value * keep + spare
                        value_ref[s, head_at : head_at + LANES] = kept[:LANES]
                        value_ref[s, tail_at : tail_at + STEP] = kept[LANES:]

    def body(block, carry):
        ahead = jnp.where(block == 1, -1, jnp.where(block == 2, 1, jnp.where(block == 3, 2, 0)))
        place = there + (place_ref[2] + ahead + count) % count

        def query_of(s):
            member = s % group
            spare = (member + 1) % group * head_size + s
            inside = (lane >= member * head_size) & (lane < (member + 1) * head_size)
            raw = own_ref[place, s // group, :residues, :].astype(F32)
            return jnp.where(inside, raw, jnp.where(lane == spare, 1.0, 0.0)).astype(BF16)

        def score(s, query, j):
            columns = slice(j * chunk, (j + 1) * chunk)
            score_ref[s % 2, :, columns] = dot_nt(query, key_ref[s, columns, :]) + bias32_ref[block, :, columns]

        def weigh(s, row):
            scores = score_ref[s % 2, row : row + TILE, :]
            top = jnp.max(scores, axis=1, keepdims=True)
            weight_ref[s % 2, row : row + TILE, :] = jnp.exp2(scores - top).astype(BF16)

        query = query_of(0)
        for j in range(keys // chunk):
            score(0, query, j)
        total = None
        for s in range(lines):
            member, pack = s % group, s // group
            query = query_of(s + 1) if s + 1 < lines else None
            steps = keys // chunk
            tiles = residues // TILE
            for j in range(steps):
                if query is not None:
                    score(s + 1, query, j)
                for r in range(j * tiles // steps, (j + 1) * tiles // steps):
                    weigh(s, r * TILE)
            mixed = dot(weight_ref[s % 2], value_ref[s])
            spare = (member + 1) % group * head_size
            mixed = mixed / mixed[:, spare : spare + 1]
            total = mixed if member == 0 else jnp.where(lane >= member * head_size, mixed, total)
            if member == group - 1:
                for piece in range(pieces):
                    part = total[piece * span : (piece + 1) * span].astype(BF16)
                    out_ref[piece, place % targets, pack * span : (pack + 1) * span, :] = part
        return carry

    lax.fori_loop(0, count, body, 0)


def row_attention(place, own, other, biases, earlier, turn, residues, pieces, head_size):
    blocks, packs, _, _ = own.shape
    lines = packs * LANES // head_size
    keys = 2 * blocks * residues
    count = len(biases)
    targets = count + sum(e.shape[1] for e in earlier)
    rows = packs * residues // pieces
    scores = lines * count * residues * keys
    return pl.pallas_call(
        functools.partial(row_kernel, turn=turn, count=count, residues=residues, head_size=head_size),
        in_specs=[pl.BlockSpec(memory_space=pltpu.SMEM)]
        + [pl.BlockSpec(memory_space=pltpu.VMEM)] * (2 + count + len(earlier)),
        out_specs=pl.BlockSpec(memory_space=pltpu.VMEM),
        out_shape=jax.ShapeDtypeStruct((pieces, targets, rows, LANES), BF16),
        scratch_shapes=[
            pltpu.VMEM((count, residues, keys), F32),
            pltpu.VMEM((lines, keys, LANES), BF16),
            pltpu.VMEM((lines, keys, LANES), BF16),
            pltpu.VMEM((2, residues, keys), F32),
            pltpu.VMEM((2, residues, keys), BF16),
        ],
        compiler_params=pltpu.CompilerParams(vmem_limit_bytes=LESS_VMEM),
        cost_estimate=pl.CostEstimate(flops=scores * 512, bytes_accessed=12_000_000, transcendentals=scores),
        name="row_attention",
    )(place, own, other, *biases, *earlier)


def column_kernel(
    mixed_ref, table_ref, mask_ref,
    row_gain_ref, row_gate_ref, row_shift_ref, row_out_ref, row_bias_ref,
    col_gain_ref, col_weight_ref, col_shift_ref, col_out_ref, col_bias_ref,
    ff_gain_ref, expand_ref, shrink_ref, out_ref, mixed32_ref, *, heads, scale,
):
    groups, span, lines, channels = table_ref.shape
    rows = groups * lines
    head_size = channels // heads

    @pl.when(pl.program_id(0) == 0)
    def _():
        members = LANES // head_size
        packs = lines // members
        received = mixed_ref.shape[2]
        residues = received // packs
        source = lax.broadcasted_iota(jnp.int32, (LANES, channels), 0)
        target = lanes_of((LANES, channels))
        tokens = [mixed_ref[:, h].astype(F32).reshape(groups * received, LANES).astype(BF16) for h in range(heads)]
        for member in range(members):
            total = None
            for h in range(heads):
                move = (target // head_size == h) & (source == target - h * head_size + member * head_size)
                part = dot(tokens[h], jnp.where(move, 1.0, 0.0).astype(BF16))
                total = part if total is None else total + part
            for r in range(groups):
                for pack in range(packs):
                    row = r * received + pack * residues
                    line = r * lines + pack * members + member
                    for part in range(channels // LANES):
                        mixed32_ref[part, pl.ds(line, residues, stride=rows), :] = total[
                            row : row + residues, part * LANES : (part + 1) * LANES
                        ]

    table = table_ref[...].astype(F32)
    table = jnp.concatenate([table[:, i].reshape(rows, channels) for i in range(span)], axis=0)
    here = pl.ds(pl.program_id(0) * span * rows, span * rows)
    mixed = jnp.concatenate([mixed32_ref[part, here, :] for part in range(channels // LANES)], axis=1)

    row_in = normalize(table, row_gain_ref[...]).astype(BF16)
    gate = jax.nn.sigmoid(dot(row_in, row_gate_ref[...]) + row_shift_ref[...])
    gated = (mixed * gate).astype(BF16)
    after_rows = table + (dot(gated, row_out_ref[...]) + row_bias_ref[...])
    after_rows = after_rows.astype(BF16).astype(F32)

    col_in = normalize(after_rows, col_gain_ref[...]).astype(BF16)
    projected = dot(col_in, col_weight_ref[...])
    query = (projected[:, :channels] * scale).astype(BF16)
    key = projected[:, channels : 2 * channels].astype(BF16)
    value = projected[:, 2 * channels : 3 * channels].astype(BF16)
    gate = jax.nn.sigmoid(projected[:, 3 * channels :] + col_shift_ref[...])

    shape = (heads * rows, channels)
    row_head = lax.broadcasted_iota(jnp.int32, shape, 0) // rows
    same = row_head == lax.broadcasted_iota(jnp.int32, shape, 1) // head_size
    same = jnp.where(same, 1.0, 0.0).astype(BF16)
    masks = mask_ref[:, 0].astype(F32).reshape(rows, channels)
    mask_lane = lanes_of((rows, channels))
    attended = []
    for i in range(span):
        here = slice(i * rows, (i + 1) * rows)
        spread_key = jnp.concatenate([key[here]] * heads, axis=0) * same
        spread_value = jnp.concatenate([value[here]] * heads, axis=0) * same
        scores = dot_nt(spread_key, query[here]).reshape(heads, rows, rows)
        place = pl.program_id(0) * span + i
        present = jnp.sum(jnp.where(mask_lane == place, masks, 0.0), axis=1, keepdims=True)
        scores = jnp.where(present[None] > 0, scores, -1e9)
        top = jnp.max(scores, axis=1, keepdims=True)
        weights = jnp.exp2(scores - top)
        weights = weights / jnp.sum(weights, axis=1, keepdims=True)
        weights = weights.astype(BF16).reshape(heads * rows, rows)
        attended.append(dot_tn(weights, spread_value))
    gated = (jnp.concatenate(attended, axis=0) * gate).astype(BF16)
    after_cols = after_rows + (dot(gated, col_out_ref[...]) + col_bias_ref[...])
    after_cols = after_cols.astype(BF16).astype(F32)

    trans_in = normalize(after_cols, ff_gain_ref[...]).astype(BF16)
    hidden = jnp.maximum(dot(trans_in, expand_ref[...]), 0.0).astype(BF16)
    updated = after_cols + dot(hidden, shrink_ref[...])
    for i in range(span):
        block = updated[i * rows : (i + 1) * rows].reshape(groups, lines, channels)
        out_ref[:, i] = block.astype(BF16)


def column_phase(mixed, table, params, heads, scale, span):
    groups, extended, lines, channels = table.shape
    residues = extended - 1
    token_block = pl.BlockSpec((groups, span, lines, channels), lambda i: (0, i, 0, 0))
    in_specs = [
        pl.BlockSpec(mixed.shape, lambda i: (0, 0, 0, 0)),
        token_block,
        pl.BlockSpec((groups, 1, lines, channels), lambda i: (0, residues, 0, 0)),
    ]
    in_specs += [pl.BlockSpec(p.shape, lambda i: (0, 0)) for p in params]
    return pl.pallas_call(
        functools.partial(column_kernel, heads=heads, scale=scale),
        grid=(residues // span,),
        in_specs=in_specs,
        out_specs=token_block,
        out_shape=jax.ShapeDtypeStruct((groups, residues, lines, channels), BF16),
        scratch_shapes=[pltpu.VMEM((channels // LANES, residues * groups * lines, LANES), F32)],
        compiler_params=pltpu.CompilerParams(vmem_limit_bytes=LESS_VMEM),
        name="column_phase",
    )(mixed, table, table, *params)


def shards(
    seq_size,
    res_size,
    homology_table,
    coupled_state,
    aligned_indicator,
    amino_indicator,
    horizontal_scaling_factor,
    horizontal_projection_matrix,
    horizontal_sigmoid_shift,
    horizontal_result_matrix,
    horizontal_result_shift,
    coupling_scaling_factor,
    coupling_head_matrix,
    downward_stretch_vector,
    vertical_projection_matrix,
    vertical_sigmoid_shift,
    vertical_result_matrix,
    vertical_result_shift,
    feedforward_scaling_factor,
    feedforward_expand_matrix,
    feedforward_shrink_matrix,
):
    lines, residues, channels = homology_table.shape
    heads = coupling_head_matrix.shape[1]
    head_size = channels // heads
    scale = LOG2E / math.sqrt(head_size)
    span = residues // seq_size
    core = lax.axis_index("res") % 2
    parity = [list(range(p, res_size, 2)) for p in (0, 1)]
    parity_all = [[r * res_size + c for r in range(seq_size) for c in group] for group in parity]

    tile_bias = pair_bias(coupled_state, coupling_scaling_factor, coupling_head_matrix, residues // STEP)
    tile_bias, homology_table = lax.optimization_barrier((tile_bias, homology_table))
    steps = tile_bias.shape[1] // 2
    near = lax.all_to_all(tile_bias.reshape(res_size, steps, STEP_ROWS, LANES), "res", 0, 0)

    by_residue = jnp.transpose(homology_table, (1, 0, 2)).reshape(seq_size, span, lines, channels)
    mask_row = jnp.transpose(aligned_indicator.reshape(lines, seq_size, span), (1, 0, 2))
    mask_row = jnp.pad(mask_row.astype(BF16), ((0, 0), (0, 0), (0, channels - span)))
    columns = jnp.concatenate([by_residue, mask_row[:, None]], axis=1)

    present = aligned_indicator * amino_indicator[None, :]
    mask = jnp.where(present > 0, 0.0, MASKED).astype(F32)
    packed = pack_heads(
        homology_table, mask, horizontal_scaling_factor, horizontal_projection_matrix, heads, scale
    )
    me = lax.axis_index("seq")
    place = jnp.stack([core, me // (seq_size // 2), me % (seq_size // 2)]).astype(jnp.int32)
    near, packed, columns, place = lax.optimization_barrier((near, packed, columns, place))
    own = lax.all_to_all(packed, "res", 0, 0, axis_index_groups=parity)

    ring = seq_size // 2

    def around(values, by):
        return lax.ppermute(
            values, "seq", [(h * ring + z, h * ring + (z + by) % ring) for h in (0, 1) for z in range(ring)]
        )

    def swap(values):
        return lax.ppermute(values, "seq", [(r, (r + ring) % seq_size) for r in range(seq_size)])

    up, down, far = around(near, 1), around(near, -1), swap(near)
    across = around(up, 1)
    own, up, down, far, across = lax.optimization_barrier((own, up, down, far, across))
    other = lax.ppermute(own, "res", [(c, c ^ 1) for c in range(res_size)])
    near_biases = [near, up, down, across]
    far_biases = [far, around(far, 1), around(far, -1), swap(across)]

    mixed = row_attention(place, own, other, near_biases, [], 0, residues, seq_size, head_size)
    columns = lax.all_to_all(columns, "seq", 0, 0)
    mixed, columns = lax.optimization_barrier((mixed, columns))
    mixed = row_attention(place, own, other, far_biases, [mixed], 1, residues, seq_size, head_size)
    mixed = mixed.reshape((seq_size * ring * 2,) + mixed.shape[2:])
    mixed = lax.all_to_all(mixed, ("seq", "res"), 0, 0, axis_index_groups=parity_all)
    mixed = mixed.reshape((seq_size, heads) + mixed.shape[1:])

    params = [
        horizontal_scaling_factor[None],
        horizontal_projection_matrix[:, 3 * channels :],
        horizontal_sigmoid_shift[None],
        horizontal_result_matrix,
        horizontal_result_shift[None],
        downward_stretch_vector[None],
        vertical_projection_matrix,
        vertical_sigmoid_shift[None],
        vertical_result_matrix,
        vertical_result_shift[None],
        feedforward_scaling_factor[None],
        feedforward_expand_matrix,
        feedforward_shrink_matrix,
    ]
    updated = column_phase(mixed, columns, params, heads, scale, span)
    updated = lax.all_to_all(updated, "seq", 0, 0)
    return jnp.transpose(updated.reshape(residues, lines, channels), (1, 0, 2))


def solution(mesh):
    table = P("seq", "res", None)
    return jax.shard_map(
        functools.partial(shards, mesh.shape["seq"], mesh.shape["res"]),
        mesh=mesh,
        in_specs=(table, table, P("seq", "res"), P("res")) + (P(),) * 15,
        out_specs=table,
        check_vma=False,
    )
```

```python
import functools
import math

import jax
import jax.numpy as jnp
from jax import lax
from jax.experimental import pallas as pl
from jax.experimental.pallas import tpu as pltpu
from jax.sharding import PartitionSpec as P

F32 = jnp.float32
BF16 = jnp.bfloat16
EPS = 1e-05
LOG2E = 1.4426950408889634
LANES = 128
MASKED = -1e30
VMEM = 56 * 2**20
LESS_VMEM = 40 * 2**20


def dot(a, b):
    return jnp.dot(a, b, preferred_element_type=F32)


def dot_nt(a, b):
    return lax.dot_general(a, b, (((1,), (1,)), ((), ())), preferred_element_type=F32)


def dot_tn(a, b):
    return lax.dot_general(a, b, (((0,), (0,)), ((), ())), preferred_element_type=F32)


def normalize(values, gain):
    center = values - jnp.mean(values, axis=-1, keepdims=True)
    spread = jnp.mean(center * center, axis=-1, keepdims=True)
    return center * lax.rsqrt(spread + EPS) * gain


def lanes_of(shape):
    return lax.broadcasted_iota(jnp.int32, shape, len(shape) - 1)


STEP = 32
GROUPS = 4
EIGHT = 8
STEP_ROWS = STEP + EIGHT


def pair_kernel(pair_ref, gain_ref, head_ref, bias_ref, project_ref, rows_ref):
    heads, channels = head_ref.shape

    @pl.when(pl.program_id(0) == 0)
    def _():
        gained = (gain_ref[...] * LOG2E) * head_ref[...].astype(F32)
        gained = gained - jnp.mean(gained, axis=1, keepdims=True)
        high = gained.astype(BF16)
        low = (gained - high.astype(F32)).astype(BF16)
        same = lax.broadcasted_iota(jnp.int32, (channels, channels), 0) == lanes_of((channels, channels))
        centering = jnp.where(same, 1.0, 0.0) - 1.0 / channels
        project_ref[:channels] = centering.astype(BF16)
        project_ref[channels:] = jnp.concatenate([high.astype(F32), low.astype(F32)], axis=0).astype(BF16)

    def project(tokens):
        both = dot_nt(project_ref[...], tokens)
        center = both[:channels]
        spread = jnp.sum(center * center, axis=0, keepdims=True) * (1.0 / channels)
        raw = both[channels : channels + heads] + both[channels + heads :]
        return raw * lax.rsqrt(spread + EPS)

    for part in range(bias_ref.shape[1]):
        row, at = part * STEP, part * STEP_ROWS
        for i in range(0, STEP, 2):
            done = project(pair_ref[row + i : row + i + 2, :LANES, :].reshape(2 * LANES, channels))
            rows_ref[:, at + i, :] = done[:, :LANES]
            rows_ref[:, at + i + 1, :] = done[:, LANES:]
        for r in range(0, EIGHT, 2):
            rest = [pair_ref[row + g * EIGHT + r + e, LANES:, :] for e in range(2) for g in range(GROUPS)]
            done = project(jnp.concatenate(rest, axis=0))
            rows_ref[:, at + STEP + r, :] = done[:, :LANES]
            rows_ref[:, at + STEP + r + 1, :] = done[:, LANES:]
    for part in range(bias_ref.shape[1]):
        bias_ref[:, part] = rows_ref[:, part * STEP_ROWS : (part + 1) * STEP_ROWS].astype(BF16)


def pair_bias(coupled, gain, head_matrix, parts):
    rows, cols, channels = coupled.shape
    heads = head_matrix.shape[1]
    return pl.pallas_call(
        pair_kernel,
        grid=(rows // STEP // parts,),
        in_specs=[
            pl.BlockSpec((parts * STEP, cols, channels), lambda i: (i, 0, 0)),
            pl.BlockSpec((1, channels), lambda i: (0, 0)),
            pl.BlockSpec((heads, channels), lambda i: (0, 0)),
        ],
        out_specs=pl.BlockSpec((heads, parts, STEP_ROWS, LANES), lambda i: (0, i, 0, 0)),
        out_shape=jax.ShapeDtypeStruct((heads, rows // STEP, STEP_ROWS, LANES), BF16),
        scratch_shapes=[
            pltpu.VMEM((channels + 2 * heads, channels), BF16),
            pltpu.VMEM((heads, parts * STEP_ROWS, LANES), F32),
        ],
        compiler_params=pltpu.CompilerParams(vmem_limit_bytes=VMEM),
        name="pair_bias",
    )(coupled, gain[None], head_matrix.T)


MASK_ROWS = 16


def pack_kernel(table_ref, mask_ref, gain_ref, weight_ref, packed_ref, *, scale):
    group, residues, channels = table_ref.shape
    heads = packed_ref.shape[0]
    head_size = channels // heads
    lane = lanes_of((residues, LANES))
    flat = []
    for member in range(group):
        normed = normalize(table_ref[member].astype(F32), gain_ref[...]).astype(BF16)
        flat.append(dot(normed, weight_ref[:, : 3 * channels]))
    for h in range(heads):
        for kind in range(3):
            column = kind * channels + h // group * LANES
            total = None
            for member in range(group):
                part = flat[member][:, column : column + LANES]
                if member != h % group:
                    part = pltpu.roll(part, ((member - h % group) * head_size) % LANES, 1)
                total = part if total is None else jnp.where(lane >= member * head_size, part, total)
            if kind == 0:
                total = total * scale
            packed_ref[h, 0, kind * residues : (kind + 1) * residues] = total.astype(BF16)
        packed_ref[h, 0, 3 * residues :] = mask_ref[0]


def pack_heads(table, mask, gain, weight, heads, scale):
    lines, residues, channels = table.shape
    group = LANES * heads // channels
    packs = lines // group
    rows = 3 * residues + MASK_ROWS
    mask = jnp.pad(mask, ((0, MASK_ROWS - lines), (0, packs * LANES - residues)))
    mask = jnp.transpose(mask.reshape(MASK_ROWS, packs, LANES), (1, 0, 2)).astype(BF16)
    return pl.pallas_call(
        functools.partial(pack_kernel, scale=scale),
        grid=(packs,),
        in_specs=[
            pl.BlockSpec((group, residues, channels), lambda s: (s, 0, 0)),
            pl.BlockSpec((1, MASK_ROWS, LANES), lambda s: (s, 0, 0)),
            pl.BlockSpec((1, channels), lambda s: (0, 0)),
            pl.BlockSpec(weight.shape, lambda s: (0, 0)),
        ],
        out_specs=pl.BlockSpec((heads, 1, rows, LANES), lambda s: (0, s, 0, 0)),
        out_shape=jax.ShapeDtypeStruct((heads, packs, rows, LANES), BF16),
        compiler_params=pltpu.CompilerParams(vmem_limit_bytes=VMEM),
        name="pack_heads",
    )(table, mask, gain[None, :], weight)


TILE = 16


def row_kernel(place_ref, own_ref, other_ref, *rest, turn, count, residues, head_size):
    bias_refs, rest = rest[:count], rest[count:]
    out_ref, bias32_ref, key_ref, value_ref, score_ref, weight_ref = rest[-6:]
    earlier = rest[:-6]
    blocks, packs, _, _ = own_ref.shape
    lines, keys, _ = key_ref.shape
    pieces, targets = out_ref.shape[:2]
    span = residues // pieces
    group = LANES // head_size
    chunk = 2 * LANES
    main = 2 * blocks * LANES
    core = place_ref[0]
    there = (place_ref[1] + turn) % 2 * count

    def place_of(number):
        return there + (place_ref[2] + (0, -1, 1, 2)[number] + count) % count

    lane8 = lanes_of((EIGHT, LANES))
    lane = lanes_of((residues, LANES))

    for ref in earlier:
        for z in range(ref.shape[1]):
            out_ref[:, place_ref[1] * count + z] = ref[:, z]

    def gather_tails(tails, at):
        total = None
        for e, moved in enumerate(tails):
            if e != at:
                moved = pltpu.roll(moved, ((e - at) * STEP) % LANES, 1)
            total = moved if total is None else jnp.where(lane8 >= e * STEP, moved, total)
        return total

    for block, ref in enumerate(bias_refs):
        for side in range(2):
            parity = core if side == 0 else 1 - core
            for step in range(residues // STEP):
                row = step * STEP
                tails = []
                for k in range(blocks):
                    tile = ref[2 * k + parity, step].astype(F32)
                    column = (side * blocks + k) * LANES
                    bias32_ref[block, row : row + STEP, column : column + LANES] = tile[:STEP]
                    tails.append(tile[STEP:])
                for q in range(blocks // GROUPS):
                    column = main + (side * blocks // GROUPS + q) * LANES
                    for g in range(GROUPS):
                        bias32_ref[block, row + g * EIGHT : row + (g + 1) * EIGHT, column : column + LANES] = (
                            gather_tails(tails[q * GROUPS : (q + 1) * GROUPS], g)
                        )

    def upright(rows):
        wide = jnp.concatenate([rows, jnp.zeros((head_size - lines, LANES), F32)] * group, axis=0)
        return wide.T.astype(BF16)

    lane1 = lanes_of((1, LANES)) // head_size
    for side, ref in enumerate((own_ref, other_ref)):
        for q in range(blocks // GROUPS):
            masks = [ref[q * GROUPS + e, :, 3 * residues :, :].astype(F32) for e in range(GROUPS)]
            rest_mask = upright(gather_tails([m[1, :lines] for m in masks], 0))
            for e in range(GROUPS):
                k = q * GROUPS + e
                first_mask = upright(masks[e][0, :lines])
                head_at = (side * blocks + k) * LANES
                tail_at = main + (side * blocks + k) * STEP
                for pack in range(packs):
                    key = ref[k, pack, residues : 2 * residues, :]
                    value = ref[k, pack, 2 * residues : 3 * residues, :]
                    for member in range(group):
                        s = pack * group + member
                        spare = jnp.where(lane1 == (member + 1) % group, 1.0, 0.0)
                        keep, spare = (1.0 - spare).astype(BF16), spare.astype(BF16)
                        kept = key * keep
                        key_ref[s, head_at : head_at + LANES] = kept[:LANES] + first_mask * spare
                        key_ref[s, tail_at : tail_at + STEP] = (
                            kept[LANES:] + rest_mask[e * STEP : (e + 1) * STEP] * spare
                        )
                        kept = value * keep + spare
                        value_ref[s, head_at : head_at + LANES] = kept[:LANES]
                        value_ref[s, tail_at : tail_at + STEP] = kept[LANES:]

    def place_at(block):
        place = place_of(0)
        for number in range(1, count):
            place = jnp.where(block == number, place_of(number), place)
        return place

    def query_of(block, s):
        member = s % group
        spare = (member + 1) % group * head_size + s
        inside = (lane >= member * head_size) & (lane < (member + 1) * head_size)
        raw = own_ref[place_at(block), s // group, :residues, :].astype(F32)
        return jnp.where(inside, raw, jnp.where(lane == spare, 1.0, 0.0)).astype(BF16)

    def score(block, s, query, j):
        columns = slice(j * chunk, (j + 1) * chunk)
        score_ref[s % 2, :, columns] = dot_nt(query, key_ref[s, columns, :]) + bias32_ref[block, :, columns]

    def body(block, carry):
        place = place_at(block)
        target = place if earlier else block
        following = jnp.minimum(block + 1, count - 1)

        def weigh(s, row):
            scores = score_ref[s % 2, row : row + TILE, :]
            top = jnp.max(scores, axis=1, keepdims=True)
            weight_ref[s % 2, row : row + TILE, :] = jnp.exp2(scores - top).astype(BF16)

        total = None
        for s in range(lines):
            member, pack = s % group, s // group
            ahead = (block, s + 1) if s + 1 < lines else (following, 0)
            query = query_of(*ahead)
            steps = keys // chunk
            tiles = residues // TILE
            for j in range(steps):
                score(*ahead, query, j)
                for r in range(j * tiles // steps, (j + 1) * tiles // steps):
                    weigh(s, r * TILE)
            mixed = dot(weight_ref[s % 2], value_ref[s])
            spare = (member + 1) % group * head_size
            mixed = mixed / mixed[:, spare : spare + 1]
            total = mixed if member == 0 else jnp.where(lane >= member * head_size, mixed, total)
            if member == group - 1:
                for piece in range(pieces):
                    part = total[piece * span : (piece + 1) * span].astype(BF16)
                    out_ref[piece, place % targets, pack * span : (pack + 1) * span, :] = part
        return carry

    query = query_of(0, 0)
    for j in range(keys // chunk):
        score(0, 0, query, j)
    lax.fori_loop(0, count, body, 0)


def row_attention(place, own, other, biases, earlier, turn, residues, pieces, head_size):
    blocks, packs, _, _ = own.shape
    lines = packs * LANES // head_size
    keys = 2 * blocks * residues
    count = len(biases)
    targets = count + sum(e.shape[1] for e in earlier)
    rows = packs * residues // pieces
    scores = lines * count * residues * keys
    return pl.pallas_call(
        functools.partial(row_kernel, turn=turn, count=count, residues=residues, head_size=head_size),
        in_specs=[pl.BlockSpec(memory_space=pltpu.SMEM)]
        + [pl.BlockSpec(memory_space=pltpu.VMEM)] * (2 + count + len(earlier)),
        out_specs=pl.BlockSpec(memory_space=pltpu.VMEM),
        out_shape=jax.ShapeDtypeStruct((pieces, targets, rows, LANES), BF16),
        scratch_shapes=[
            pltpu.VMEM((count, residues, keys), F32),
            pltpu.VMEM((lines, keys, LANES), BF16),
            pltpu.VMEM((lines, keys, LANES), BF16),
            pltpu.VMEM((2, residues, keys), F32),
            pltpu.VMEM((2, residues, keys), BF16),
        ],
        compiler_params=pltpu.CompilerParams(vmem_limit_bytes=LESS_VMEM),
        cost_estimate=pl.CostEstimate(flops=scores * 512, bytes_accessed=12_000_000, transcendentals=scores),
        name="row_attention",
    )(place, own, other, *biases, *earlier)


def column_kernel(
    mixed_ref, table_ref, mask_ref,
    row_gain_ref, row_gate_ref, row_shift_ref, row_out_ref, row_bias_ref,
    col_gain_ref, col_weight_ref, col_shift_ref, col_out_ref, col_bias_ref,
    ff_gain_ref, expand_ref, shrink_ref, out_ref, mixed32_ref, *, heads, scale,
):
    groups, span, lines, channels = table_ref.shape
    rows = groups * lines
    head_size = channels // heads

    @pl.when(pl.program_id(0) == 0)
    def _():
        members = LANES // head_size
        packs = lines // members
        received = mixed_ref.shape[2]
        residues = received // packs
        source = lax.broadcasted_iota(jnp.int32, (LANES, channels), 0)
        target = lanes_of((LANES, channels))
        tokens = [mixed_ref[:, h].astype(F32).reshape(groups * received, LANES).astype(BF16) for h in range(heads)]
        for member in range(members):
            total = None
            for h in range(heads):
                move = (target // head_size == h) & (source == target - h * head_size + member * head_size)
                part = dot(tokens[h], jnp.where(move, 1.0, 0.0).astype(BF16))
                total = part if total is None else total + part
            for r in range(groups):
                for pack in range(packs):
                    row = r * received + pack * residues
                    line = r * lines + pack * members + member
                    for part in range(channels // LANES):
                        mixed32_ref[part, pl.ds(line, residues, stride=rows), :] = total[
                            row : row + residues, part * LANES : (part + 1) * LANES
                        ]

    table = table_ref[...].astype(F32)
    table = jnp.concatenate([table[:, i].reshape(rows, channels) for i in range(span)], axis=0)
    here = pl.ds(pl.program_id(0) * span * rows, span * rows)
    mixed = jnp.concatenate([mixed32_ref[part, here, :] for part in range(channels // LANES)], axis=1)

    row_in = normalize(table, row_gain_ref[...]).astype(BF16)
    gate = jax.nn.sigmoid(dot(row_in, row_gate_ref[...]) + row_shift_ref[...])
    gated = (mixed * gate).astype(BF16)
    after_rows = table + (dot(gated, row_out_ref[...]) + row_bias_ref[...])
    after_rows = after_rows.astype(BF16).astype(F32)

    col_in = normalize(after_rows, col_gain_ref[...]).astype(BF16)
    projected = dot(col_in, col_weight_ref[...])
    query = (projected[:, :channels] * scale).astype(BF16)
    key = projected[:, channels : 2 * channels].astype(BF16)
    value = projected[:, 2 * channels : 3 * channels].astype(BF16)
    gate = jax.nn.sigmoid(projected[:, 3 * channels :] + col_shift_ref[...])

    shape = (heads * rows, channels)
    row_head = lax.broadcasted_iota(jnp.int32, shape, 0) // rows
    same = row_head == lax.broadcasted_iota(jnp.int32, shape, 1) // head_size
    same = jnp.where(same, 1.0, 0.0).astype(BF16)
    masks = mask_ref[:, 0].astype(F32).reshape(rows, channels)
    mask_lane = lanes_of((rows, channels))
    attended = []
    for i in range(span):
        here = slice(i * rows, (i + 1) * rows)
        spread_key = jnp.concatenate([key[here]] * heads, axis=0) * same
        spread_value = jnp.concatenate([value[here]] * heads, axis=0) * same
        scores = dot_nt(spread_key, query[here]).reshape(heads, rows, rows)
        place = pl.program_id(0) * span + i
        present = jnp.sum(jnp.where(mask_lane == place, masks, 0.0), axis=1, keepdims=True)
        scores = jnp.where(present[None] > 0, scores, -1e9)
        top = jnp.max(scores, axis=1, keepdims=True)
        weights = jnp.exp2(scores - top)
        weights = weights * (1.0 / jnp.sum(weights, axis=1, keepdims=True))
        weights = weights.astype(BF16).reshape(heads * rows, rows)
        attended.append(dot_tn(weights, spread_value))
    gated = (jnp.concatenate(attended, axis=0) * gate).astype(BF16)
    after_cols = after_rows + (dot(gated, col_out_ref[...]) + col_bias_ref[...])
    after_cols = after_cols.astype(BF16).astype(F32)

    trans_in = normalize(after_cols, ff_gain_ref[...]).astype(BF16)
    hidden = jnp.maximum(dot(trans_in, expand_ref[...]), 0.0).astype(BF16)
    updated = after_cols + dot(hidden, shrink_ref[...])
    for i in range(span):
        block = updated[i * rows : (i + 1) * rows].reshape(groups, lines, channels)
        out_ref[:, i] = block.astype(BF16)


def column_phase(mixed, table, params, heads, scale, span):
    groups, extended, lines, channels = table.shape
    residues = extended - 1
    token_block = pl.BlockSpec((groups, span, lines, channels), lambda i: (0, i, 0, 0))
    in_specs = [
        pl.BlockSpec(mixed.shape, lambda i: (0, 0, 0, 0)),
        token_block,
        pl.BlockSpec((groups, 1, lines, channels), lambda i: (0, residues, 0, 0)),
    ]
    in_specs += [pl.BlockSpec(p.shape, lambda i: (0, 0)) for p in params]
    return pl.pallas_call(
        functools.partial(column_kernel, heads=heads, scale=scale),
        grid=(residues // span,),
        in_specs=in_specs,
        out_specs=token_block,
        out_shape=jax.ShapeDtypeStruct((groups, residues, lines, channels), BF16),
        scratch_shapes=[pltpu.VMEM((channels // LANES, residues * groups * lines, LANES), F32)],
        compiler_params=pltpu.CompilerParams(vmem_limit_bytes=LESS_VMEM),
        name="column_phase",
    )(mixed, table, table, *params)


def shards(
    seq_size,
    res_size,
    homology_table,
    coupled_state,
    aligned_indicator,
    amino_indicator,
    horizontal_scaling_factor,
    horizontal_projection_matrix,
    horizontal_sigmoid_shift,
    horizontal_result_matrix,
    horizontal_result_shift,
    coupling_scaling_factor,
    coupling_head_matrix,
    downward_stretch_vector,
    vertical_projection_matrix,
    vertical_sigmoid_shift,
    vertical_result_matrix,
    vertical_result_shift,
    feedforward_scaling_factor,
    feedforward_expand_matrix,
    feedforward_shrink_matrix,
):
    lines, residues, channels = homology_table.shape
    heads = coupling_head_matrix.shape[1]
    head_size = channels // heads
    scale = LOG2E / math.sqrt(head_size)
    span = residues // seq_size
    core = lax.axis_index("res") % 2
    parity = [list(range(p, res_size, 2)) for p in (0, 1)]
    parity_all = [[r * res_size + c for r in range(seq_size) for c in group] for group in parity]

    tile_bias = pair_bias(coupled_state, coupling_scaling_factor, coupling_head_matrix, residues // STEP)
    tile_bias, homology_table = lax.optimization_barrier((tile_bias, homology_table))
    steps = tile_bias.shape[1] // 2
    near = lax.all_to_all(tile_bias.reshape(res_size, steps, STEP_ROWS, LANES), "res", 0, 0)

    by_residue = jnp.transpose(homology_table, (1, 0, 2)).reshape(seq_size, span, lines, channels)
    mask_row = jnp.transpose(aligned_indicator.reshape(lines, seq_size, span), (1, 0, 2))
    mask_row = jnp.pad(mask_row.astype(BF16), ((0, 0), (0, 0), (0, channels - span)))
    columns = jnp.concatenate([by_residue, mask_row[:, None]], axis=1)

    present = aligned_indicator * amino_indicator[None, :]
    mask = jnp.where(present > 0, 0.0, MASKED).astype(F32)
    packed = pack_heads(
        homology_table, mask, horizontal_scaling_factor, horizontal_projection_matrix, heads, scale
    )
    me = lax.axis_index("seq")
    place = jnp.stack([core, me // (seq_size // 2), me % (seq_size // 2)]).astype(jnp.int32)
    near, packed, columns, place = lax.optimization_barrier((near, packed, columns, place))
    own = lax.all_to_all(packed, "res", 0, 0, axis_index_groups=parity)

    ring = seq_size // 2

    def around(values, by):
        return lax.ppermute(
            values, "seq", [(h * ring + z, h * ring + (z + by) % ring) for h in (0, 1) for z in range(ring)]
        )

    def swap(values):
        return lax.ppermute(values, "seq", [(r, (r + ring) % seq_size) for r in range(seq_size)])

    up, down, far = around(near, 1), around(near, -1), swap(near)
    across = around(up, 1)
    own, up, down, far, across = lax.optimization_barrier((own, up, down, far, across))
    other = lax.ppermute(own, "res", [(c, c ^ 1) for c in range(res_size)])
    near_biases = [near, up, down, across]
    far_biases = [far, around(far, 1), around(far, -1), swap(across)]

    mixed = row_attention(place, own, other, near_biases, [], 0, residues, seq_size, head_size)
    columns = lax.all_to_all(columns, "seq", 0, 0)
    mixed, columns = lax.optimization_barrier((mixed, columns))
    mixed = row_attention(place, own, other, far_biases, [mixed], 1, residues, seq_size, head_size)
    mixed = mixed.reshape((seq_size * ring * 2,) + mixed.shape[2:])
    mixed = lax.all_to_all(mixed, ("seq", "res"), 0, 0, axis_index_groups=parity_all)
    mixed = mixed.reshape((seq_size, heads) + mixed.shape[1:])

    params = [
        horizontal_scaling_factor[None],
        horizontal_projection_matrix[:, 3 * channels :],
        horizontal_sigmoid_shift[None],
        horizontal_result_matrix,
        horizontal_result_shift[None],
        downward_stretch_vector[None],
        vertical_projection_matrix,
        vertical_sigmoid_shift[None],
        vertical_result_matrix,
        vertical_result_shift[None],
        feedforward_scaling_factor[None],
        feedforward_expand_matrix,
        feedforward_shrink_matrix,
    ]
    updated = column_phase(mixed, columns, params, heads, scale, span)
    updated = lax.all_to_all(updated, "seq", 0, 0)
    return jnp.transpose(updated.reshape(residues, lines, channels), (1, 0, 2))


def solution(mesh):
    table = P("seq", "res", None)
    return jax.shard_map(
        functools.partial(shards, mesh.shape["seq"], mesh.shape["res"]),
        mesh=mesh,
        in_specs=(table, table, P("seq", "res"), P("res")) + (P(),) * 15,
        out_specs=table,
        check_vma=False,
    )
```
